128 devices in a mesh: mesh: 8 (over x, core), chan: 16 (over z, y).
Axes of the slice: x: 4, y: 4, z: 4, core: 2. Of those that a mesh axis runs over, the one named last changes fastest.
Arguments:
- node_latents: bfloat16 [16384, 512], P(('mesh', 'chan')), may hold values from -6 to 6
- edge_latents: bfloat16 [131072, 512], P(('mesh', 'chan')), may hold values from -6 to 6
- sender_slot: int32 [131072], P(('mesh', 'chan')), may hold values from 0 to 2175, as said below
- receiver_node: int32 [131072], P(('mesh', 'chan')), may hold values from 0 to 127, as said below
- send_rows: int32 [16384, 16], P(('mesh', 'chan')), may hold values from 0 to 127
- edge_in: bfloat16 [2, 3, 512, 512], P(None, None, 'chan'), may hold values from -0.15625 to 0.15625
- edge_out: bfloat16 [2, 512, 512], P(None, 'chan'), may hold values from -0.25 to 0.25
- node_in: bfloat16 [2, 2, 512, 512], P(None, None, 'chan'), may hold values from -0.1875 to 0.1875
- node_out: bfloat16 [2, 512, 512], P(None, 'chan'), may hold values from -0.25 to 0.25
Outputs:
- node_state: bfloat16 [16384, 512], P(('mesh', 'chan'))
- edge_state: bfloat16 [131072, 512], P(('mesh', 'chan'))
The draws below stay inside these ranges and needn't reach their ends.
Inputs may be any that keep to these rules, and one draw needn't show every extreme that they name: `sender_slot`: below 128 a node of the edge's own device; 128 + p * 16 + s names slot s of what device p sends to the edge's device, p never the device itself; both ends of the range occur in every draw. `receiver_node`: sorted within each device's 1024 edges.
All inputs are finite; a program needn't handle non-finite values.
Results may differ from the reference program's by a relative error of at most 0.014.
Values may be sent and summed in bfloat16 or wider, within the bound.
A program may use at most 64 MiB of HBM per device.

```python
import jax
import jax.numpy as jnp
from jax import lax

D = 512
NODE_DEV = 128
EDGE_DEV = 1024
SLOT = 16
ROUNDS = 2
NODES = 16384
EDGES = 131072
DEVICES = 128


def draw_sender_slot(key, part):
    key = jax.random.fold_in(key, 11)
    key_peer, key_count, key_slot, key_own, key_far = jax.random.split(key, 5)
    device = jnp.arange(EDGES, dtype=jnp.int32) // EDGE_DEV
    offset = jax.random.randint(key_peer, (EDGES,), 1, DEVICES)
    peer_index = (device + offset) % DEVICES
    capacity = jax.random.randint(key_count, (DEVICES, DEVICES), 1, SLOT + 1)
    rows_iota = jnp.arange(DEVICES, dtype=jnp.int32)
    neighbour = rows_iota[:, None] == (rows_iota[None, :] + 1) % DEVICES
    capacity = jnp.where(neighbour, SLOT, capacity)
    live_count = capacity[peer_index, device]
    slot_index = jax.random.randint(key_slot, (EDGES,), 0, 1 << 20) % live_count
    own_node = jax.random.randint(key_own, (EDGES,), 0, NODE_DEV)
    is_remote = jax.random.randint(key_far, (EDGES,), 0, 2) == 1
    drawn = jnp.where(is_remote, NODE_DEV + peer_index * SLOT + slot_index, own_node).astype(jnp.int32)
    drawn = drawn.at[0].set(0)
    drawn = drawn.at[(DEVICES - 2) * EDGE_DEV].set(NODE_DEV + DEVICES * SLOT - 1)
    return drawn.astype(jnp.int32)


def draw_receiver_node(key, part):
    key = jax.random.fold_in(key, 23)
    drawn = jax.random.randint(key, (DEVICES, EDGE_DEV), 0, NODE_DEV)
    drawn = jnp.sort(drawn, axis=1)
    drawn = drawn.at[:, 0].set(0)
    drawn = drawn.at[:, EDGE_DEV - 1].set(NODE_DEV - 1)
    return drawn.reshape(EDGES).astype(jnp.int32)


def place_ends(array, rng, low, top_value):
    spot = [jax.random.randint(jax.random.fold_in(rng, axis), (), 0, length) for axis, length in enumerate(array.shape)]
    widest = array.shape.index(max(array.shape))
    beside = spot[:widest] + [(spot[widest] + 1) % array.shape[widest]] + spot[widest + 1:]
    return array.at[tuple(spot)].set(low).at[tuple(beside)].set(top_value)


def block_scale(rng, dims, cuts, smallest, high):
    def one(axis_at, blocks):
        steps = jax.random.uniform(jax.random.fold_in(jax.random.fold_in(rng, 6), axis_at), (blocks,), jnp.float32, smallest / len(cuts), high / len(cuts))
        return jnp.repeat(jnp.exp(steps), dims[axis_at] // blocks).reshape((-1,) + (1,) * (len(dims) - axis_at - 1))

    loudness = one(*cuts[0])
    for cut in cuts[1:]:
        loudness = loudness * one(*cut)
    return loudness


def gaussian(own_key, shape, deviation, most, cuts=(), held_as=jnp.bfloat16):
    gain = block_scale(own_key, shape, cuts, -0.22, 0.18) if cuts else 1.0
    array = jax.random.normal(own_key, shape, jnp.float32) * deviation * gain
    return jnp.minimum(jnp.maximum(array, -most), most).astype(held_as)


def setup_inputs(seed: int = 0) -> dict:
    key_list = jax.random.split(jax.random.key(seed), 10)
    return {
        "node_latents": gaussian(key_list[0], (NODES, D), 1.0, 6.0, ((0, 128),)),
        "edge_latents": gaussian(key_list[1], (EDGES, D), 1.0, 6.0, ((0, 128),)),
        "sender_slot": draw_sender_slot(jax.random.fold_in(key_list[9], 71), 0),
        "receiver_node": draw_receiver_node(jax.random.fold_in(key_list[9], 71), 0),
        "send_rows": place_ends(jax.random.randint(key_list[4], (DEVICES * DEVICES, SLOT), 0, NODE_DEV), jax.random.fold_in(key_list[4], 1), 0, NODE_DEV - 1).astype(jnp.int32),
        "edge_in": gaussian(key_list[5], (ROUNDS, 3, D, D), (3 * D) ** -0.5, 0.15625, ((2, 16),)),
        "edge_out": gaussian(key_list[6], (ROUNDS, D, D), D ** -0.5, 0.25, ((1, 16),)),
        "node_in": gaussian(key_list[7], (ROUNDS, 2, D, D), (2 * D) ** -0.5, 0.1875, ((2, 16),)),
        "node_out": gaussian(key_list[8], (ROUNDS, D, D), D ** -0.5, 0.25, ((1, 16),)),
    }


def norm_rows(output):
    row_mean = lax.optimization_barrier(jnp.sum(output, axis=1, keepdims=True)) / D
    row_square = lax.optimization_barrier(jnp.sum(output * output, axis=1, keepdims=True)) / D
    return (output - row_mean) * lax.rsqrt(row_square - row_mean * row_mean + 1e-05)

def reference(node_latents, edge_latents, sender_slot, receiver_node, send_rows, edge_in, edge_out, node_in, node_out):
    device = (jnp.arange(EDGES, dtype=jnp.int32) // EDGE_DEV).astype(jnp.int32)
    far_rows = jnp.maximum(sender_slot - NODE_DEV, 0).astype(jnp.int32)
    peer_index = (far_rows // SLOT).astype(jnp.int32)
    slot_index = (far_rows % SLOT).astype(jnp.int32)
    remote_node = send_rows[peer_index * DEVICES + device, slot_index]
    senders = jnp.where(sender_slot < NODE_DEV, device * NODE_DEV + sender_slot, peer_index * NODE_DEV + remote_node).astype(jnp.int32)
    receivers = (device * NODE_DEV + receiver_node).astype(jnp.int32)
    node_state = node_latents
    edge_state = edge_latents
    for round_index in range(ROUNDS):
        send_proj = jnp.dot(node_state, edge_in[round_index, 1], preferred_element_type=jnp.float32).astype(jnp.bfloat16)
        recv_proj = jnp.dot(node_state, edge_in[round_index, 2], preferred_element_type=jnp.float32).astype(jnp.bfloat16)
        preact = jnp.dot(edge_state, edge_in[round_index, 0], preferred_element_type=jnp.float32)
        preact = preact + send_proj[senders].astype(jnp.float32) + recv_proj[receivers].astype(jnp.float32)
        edge_hidden = jax.nn.silu(preact).astype(jnp.bfloat16)
        output = jnp.dot(edge_hidden, edge_out[round_index], preferred_element_type=jnp.float32)
        edge_state = (edge_state.astype(jnp.float32) + norm_rows(output)).astype(jnp.bfloat16)
        aggregate = jax.ops.segment_sum(edge_state.astype(jnp.float32), receivers, num_segments=NODES).astype(jnp.bfloat16)
        preact = jnp.dot(node_state, node_in[round_index, 0], preferred_element_type=jnp.float32)
        preact = preact + jnp.dot(aggregate, node_in[round_index, 1], preferred_element_type=jnp.float32)
        node_hidden = jax.nn.silu(preact).astype(jnp.bfloat16)
        output = jnp.dot(node_hidden, node_out[round_index], preferred_element_type=jnp.float32)
        node_state = (node_state.astype(jnp.float32) + norm_rows(output)).astype(jnp.bfloat16)
    return (node_state, edge_state)
```

```python
import functools

import jax
import jax.numpy as jnp
from jax import lax
from jax.experimental import pallas as pl
from jax.experimental.pallas import tpu as pltpu
from jax.sharding import PartitionSpec as P

MESH = pl.DeviceIdType.MESH
F32 = jnp.float32
BF16 = jnp.bfloat16
WIDTH = 512
NODE = 128
EDGE = 1024
DEVICES = 128
SLOT = 16
TILE = 512
GROUPS = ((0, 4), (4, 7))


def mm(a, b):
    return jnp.dot(a, b, preferred_element_type=F32)


def norm_rows(v):
    mean = jnp.sum(v, axis=1, keepdims=True) * (1.0 / WIDTH)
    square = jnp.sum(v * v, axis=1, keepdims=True) * (1.0 / WIDTH)
    return (v - mean) * lax.rsqrt(square - mean * mean + 1e-05)


def silu(v):
    return v / (1.0 + jnp.exp(-v))


def kernel(
    node_ref, edge_ref, sender_ref, receiver_ref, rows_ref, ein, eout, nin, nout,
    node_out_ref, edge_out_ref,
    weights, outgoing, table, pick_sender, pick_receiver, sum_receiver, pick_send, base, aggregate,
    ready, load_sem, ex_send, ex_recv, p1s, p1r, p2s, p2r, d1s, d1r, d2s, d2r,
):
    m = lax.axis_index("mesh")
    c = lax.axis_index("chan")
    me = m * 16 + c
    x, core = m // 2, lax.rem(m, 2)
    z, y = c // 4, lax.rem(c, 4)
    sibling = (x * 2 + 1 - core, c)

    barrier = pltpu.get_barrier_semaphore()

    def greet_line(k, carry):
        pl.semaphore_signal(barrier, inc=1, device_id=(lax.rem(m + k, 8), c), device_id_type=MESH)
        return carry

    def greet_plane(sem):
        def step(k, carry):
            pl.semaphore_signal(sem, inc=1, device_id=(m, lax.rem(c + k, 16)), device_id_type=MESH)
            return carry
        lax.fori_loop(1, 16, step, 0)

    lax.fori_loop(1, 8, greet_line, 0)
    greet_plane(barrier)

    for r in range(2):
        for src, low, high in ((ein.at[r], 0, 3), (eout.at[pl.ds(r, 1)], 3, 4), (nin.at[r], 4, 6), (nout.at[pl.ds(r, 1)], 6, 7)):
            pltpu.make_async_copy(src, weights.at[r, low:high, z, y], load_sem.at[r]).start()

    sub = lax.broadcasted_iota(jnp.int32, (128, 128), 0)
    lane = lax.broadcasted_iota(jnp.int32, (128, 128), 1)
    lane_f = lane.astype(F32)
    eye = sub == lane
    ones = jnp.ones((128, 128), BF16)

    def column(row):
        wide = jnp.broadcast_to(row.astype(F32), (128, 128))
        return mm(jnp.where(eye, wide, 0.0).astype(BF16), ones)

    def hot(mask):
        return jnp.where(mask, 1.0, 0.0).astype(BF16)

    slots = rows_ref[...].astype(F32).astype(BF16)

    def send_block(b, carry):
        spread = mm(hot(lane == 8 * b + sub // SLOT), slots)
        at = lax.broadcasted_iota(jnp.int32, (128, SLOT), 1) == lax.rem(lax.broadcasted_iota(jnp.int32, (128, SLOT), 0), SLOT)
        index = jnp.sum(jnp.where(at, spread, 0.0), axis=1, keepdims=True)
        pick = hot(index == lane_f)
        rows = pl.ds(pl.multiple_of(b * 128, 128), 128)
        pick_send[rows, :] = pick
        outgoing[rows, :] = mm(pick, node_ref[...]).astype(BF16)
        return carry

    lax.fori_loop(0, 16, send_block, 0)
    table[0, pl.ds(pl.multiple_of(me * SLOT, SLOT), SLOT), :] = jnp.zeros((SLOT, WIDTH), BF16)
    table[1, pl.ds(pl.multiple_of(me * SLOT, SLOT), SLOT), :] = jnp.zeros((SLOT, WIDTH), BF16)

    def wait_load(r):
        pltpu.make_async_copy(weights.at[r, :, z, y], weights.at[r, :, z, y], load_sem.at[r]).wait()

    def remote(src, send, recv, device):
        return pltpu.make_async_remote_copy(
            src_ref=src, dst_ref=src, send_sem=send, recv_sem=recv, device_id=device, device_id_type=MESH
        )

    def at(pos, k):
        return lax.rem(pos + k + 4, 4)

    def phase1(r, g, k):
        low, high = GROUPS[g]
        to = (m, 4 * z + at(y, k)) if g == 0 else (m, 4 * at(z, k) + y)
        return remote(weights.at[r, low:high, z, y, core], p1s.at[r, g, k - 1], p1r.at[r, g, k - 1], to)

    def side1(r, g, k):
        low, high = GROUPS[g]
        if g == 0:
            src = weights.at[r, low:high, z, at(y, -k), core]
        else:
            src = weights.at[r, low:high, at(z, -k), y, core]
        return remote(src, d1s.at[r, g, k - 1], d1r.at[r, g, k - 1], sibling)

    def phase2(r, g, k):
        low, high = GROUPS[g]
        if g == 0:
            return remote(weights.at[r, low:high, z, :, core], p2s.at[r, g, k - 1], p2r.at[r, g, k - 1], (m, 4 * at(z, k) + y))
        return remote(weights.at[r, low:high, :, y, core], p2s.at[r, g, k - 1], p2r.at[r, g, k - 1], (m, 4 * z + at(y, k)))

    def side2(r, g, k):
        low, high = GROUPS[g]
        if g == 0:
            src = weights.at[r, low:high, at(z, -k), :, core]
        else:
            src = weights.at[r, low:high, :, at(y, -k), core]
        return remote(src, d2s.at[r, g, k - 1], d2r.at[r, g, k - 1], sibling)

    def start_phase1(r):
        wait_load(r)
        for g in range(2):
            for k in (1, 3, 2):
                phase1(r, g, k).start()

    def start_phase2(r):
        for g in range(2):
            for k in (1, 2, 3):
                phase1(r, g, k).wait_recv()
            for k in (1, 3, 2):
                phase2(r, g, k).start()
            for k in (1, 2, 3):
                side1(r, g, k).start()

    def start_side2(r):
        for g in range(2):
            for k in (1, 2, 3):
                phase2(r, g, k).wait_recv()
                side2(r, g, k).start()

    def wait_side(r, g):
        for k in (1, 2, 3):
            side1(r, g, k).wait_recv()
            side2(r, g, k).wait_recv()

    def start_exchange(r):
        def step(k, carry):
            p = lax.rem(me + k, DEVICES)
            pltpu.make_async_remote_copy(
                src_ref=outgoing.at[pl.ds(pl.multiple_of(p * SLOT, SLOT), SLOT)],
                dst_ref=table.at[r, pl.ds(pl.multiple_of(me * SLOT, SLOT), SLOT)],
                send_sem=ex_send.at[r], recv_sem=ex_recv.at[r],
                device_id=(p // 16, lax.rem(p, 16)), device_id_type=MESH,
            ).start()
            return carry
        lax.fori_loop(1, DEVICES, step, 0)

    def exchange_bytes(sem):
        part = pl.ds(0, (DEVICES - 1) * SLOT)
        return pltpu.make_async_copy(outgoing.at[part], outgoing.at[part], sem)

    def matrix(r, i):
        return weights[r, i].reshape(WIDTH, WIDTH)

    pl.semaphore_wait(barrier, 22)
    greet_plane(ready)
    start_phase1(0)

    def edge_block(i, carry):
        rows = pl.ds(pl.multiple_of(i * 128, 128), 128)
        sender = sender_ref[pl.ds(i, 1), :]
        receiver = receiver_ref[pl.ds(i, 1), :]
        index = column(lax.shift_right_logical(sender, 7)) * 128.0 + column(sender & 127)
        for j in range(17):
            pick_sender[rows, j * 128:(j + 1) * 128] = hot(index == lane_f + 128.0 * j)
        pick_receiver[rows, :] = hot(column(receiver) == lane_f)
        sum_receiver[:, rows] = hot(receiver == sub)
        return carry

    pl.semaphore_wait(ready, 15)
    start_exchange(0)
    lax.fori_loop(0, 8, edge_block, 0)
    start_phase2(0)
    start_side2(0)
    start_phase1(1)

    for r in range(2):
        nodes = node_ref if r == 0 else node_out_ref
        edges = edge_ref if r == 0 else edge_out_ref
        wait_side(r, 0)

        recv_proj = mm(nodes[...], matrix(r, 2)).astype(BF16)

        def before(t, carry):
            rows = pl.ds(pl.multiple_of(t * TILE, TILE), TILE)
            base[rows, :] = mm(edges[rows, :], matrix(r, 0)) + mm(pick_receiver[rows, :], recv_proj)
            return carry

        lax.fori_loop(0, EDGE // TILE, before, 0)
        exchange_bytes(ex_recv.at[r]).wait()
        if r == 0:
            start_phase2(1)

        def after(t, carry):
            rows = pl.ds(pl.multiple_of(t * TILE, TILE), TILE)
            gathered = mm(pick_sender[rows, 0:128], nodes[...]) + mm(pick_sender[rows, 128:2176], table[r])
            preact = base[rows, :] + mm(gathered.astype(BF16), matrix(r, 1))
            output = mm(silu(preact).astype(BF16), matrix(r, 3))
            edge_out_ref[rows, :] = (edges[rows, :].astype(F32) + norm_rows(output)).astype(BF16)
            return carry

        lax.fori_loop(0, EDGE // TILE, after, 0)
        if r == 0:
            start_side2(1)
        wait_side(r, 1)
        total = mm(sum_receiver[...], edge_out_ref[...]).astype(BF16)
        preact = mm(nodes[...], matrix(r, 4)) + mm(total, matrix(r, 5))
        output = mm(silu(preact).astype(BF16), matrix(r, 6))
        node_out_ref[...] = (nodes[...].astype(F32) + norm_rows(output)).astype(BF16)
        exchange_bytes(ex_send.at[r]).wait()
        if r == 0:
            def resend(b, carry):
                rows = pl.ds(pl.multiple_of(b * 512, 512), 512)
                outgoing[rows, :] = mm(pick_send[rows, :], node_out_ref[...]).astype(BF16)
                return carry
            lax.fori_loop(0, 4, resend, 0)
            start_exchange(1)

    for r in range(2):
        for g in range(2):
            for k in (1, 2, 3):
                phase1(r, g, k).wait_send()
                phase2(r, g, k).wait_send()
                side1(r, g, k).wait_send()
                side2(r, g, k).wait_send()


def local(node_latents, edge_latents, sender_slot, receiver_node, send_rows, edge_in, edge_out, node_in, node_out):
    vmem = pl.BlockSpec(memory_space=pltpu.VMEM)
    anywhere = pl.BlockSpec(memory_space=pl.ANY)
    dma = pltpu.SemaphoreType.DMA
    return pl.pallas_call(
        kernel,
        out_shape=(
            jax.ShapeDtypeStruct((NODE, WIDTH), BF16),
            jax.ShapeDtypeStruct((EDGE, WIDTH), BF16),
        ),
        in_specs=[vmem] * 5 + [anywhere] * 4,
        out_specs=(vmem, vmem),
        scratch_shapes=[
            pltpu.VMEM((2, 7, 4, 4, 2, 16, WIDTH), BF16),
            pltpu.VMEM((DEVICES * SLOT, WIDTH), BF16),
            pltpu.VMEM((2, DEVICES * SLOT, WIDTH), BF16),
            pltpu.VMEM((EDGE, NODE + DEVICES * SLOT), BF16),
            pltpu.VMEM((EDGE, NODE), BF16),
            pltpu.VMEM((NODE, EDGE), BF16),
            pltpu.VMEM((DEVICES * SLOT, NODE), BF16),
            pltpu.VMEM((EDGE, WIDTH), F32),
            pltpu.VMEM((NODE, WIDTH), F32),
            pltpu.SemaphoreType.REGULAR,
            dma((2,)), dma((2,)), dma((2,)),
        ] + [dma((2, 2, 3))] * 8,
        compiler_params=pltpu.CompilerParams(
            collective_id=0, has_side_effects=True, vmem_limit_bytes=56 * 1024 * 1024
        ),
    )(
        node_latents,
        edge_latents,
        sender_slot.reshape(8, 128),
        receiver_node.reshape(8, 128),
        send_rows,
        edge_in.reshape(2, 3, 2, 16, WIDTH),
        edge_out.reshape(2, 2, 16, WIDTH),
        node_in.reshape(2, 2, 2, 16, WIDTH),
        node_out.reshape(2, 2, 16, WIDTH),
    )


def solution(mesh):
    rows = P(("mesh", "chan"), None)
    flat = P(("mesh", "chan"))
    return jax.shard_map(
        local,
        mesh=mesh,
        in_specs=(
            rows, rows, flat, flat, rows,
            P(None, None, "chan", None), P(None, "chan", None),
            P(None, None, "chan", None), P(None, "chan", None),
        ),
        out_specs=(rows, rows),
        check_vma=False,
    )
```

```python
import jax
import jax.numpy as jnp
from jax import lax
from jax.experimental import pallas as pl
from jax.experimental.pallas import tpu as pltpu
from jax.sharding import PartitionSpec as P

MESH = pl.DeviceIdType.MESH
F32 = jnp.float32
BF16 = jnp.bfloat16
WIDTH = 512
NODE = 128
EDGE = 1024
SLOT = 16
PLANE = 32
PLANE_ROWS = PLANE * SLOT
TILE = 512
PARTS = ((0, 4), (4, 7))
ORDER = (1, 3, 2)


def mm(a, b):
    return jnp.dot(a, b, preferred_element_type=F32)


def hot(mask):
    return jnp.where(mask, 1.0, 0.0).astype(BF16)


def norm_rows(v):
    mean = jnp.sum(v, axis=1, keepdims=True) * (1.0 / WIDTH)
    square = jnp.sum(v * v, axis=1, keepdims=True) * (1.0 / WIDTH)
    return (v - mean) * lax.rsqrt(square - mean * mean + 1e-05)


def silu(v):
    return v / (1.0 + jnp.exp(-v))


def kernel(
    node_ref, edge_ref, sender_ref, receiver_ref, slots_ref, ein, eout, nin, nout,
    node_out_ref, edge_out_ref,
    weights, outgoing, table, node_mid, line_nodes, own_slots, line_slots,
    pick_local, pick_sender, pick_receiver, sum_receiver, pick_send, base, gathered,
    load_sem, ex_send, ex_recv, node_send, node_recv, slot_send, slot_recv,
    plane_send, plane_recv, line_send, line_recv, side_send, side_recv,
):
    m = lax.axis_index("mesh")
    c = lax.axis_index("chan")
    x, core = m // 2, lax.rem(m, 2)
    own = core * 16 + c
    sibling = (x * 2 + 1 - core, c)

    def along(k):
        return lax.rem(x + k + 4, 4)

    def line(k):
        return (along(k) * 2 + core, c)

    def peer(j):
        q = lax.rem(own + j, PLANE)
        return q, (x * 2 + q // 16, lax.rem(q, 16))

    barrier = pltpu.get_barrier_semaphore()
    for k in ORDER:
        pl.semaphore_signal(barrier, inc=1, device_id=line(k), device_id_type=MESH)

    def greet(j, carry):
        pl.semaphore_signal(barrier, inc=1, device_id=peer(j)[1], device_id_type=MESH)
        return carry

    lax.fori_loop(1, PLANE, greet, 0)

    columns = pl.ds(pl.multiple_of(x * 128, 128), 128)
    for r in range(2):
        for src, low, high in (
            (ein.at[r, :, core, :, columns], 0, 3),
            (eout.at[pl.ds(r, 1), core, :, columns], 3, 4),
            (nin.at[r, :, core, :, columns], 4, 6),
            (nout.at[pl.ds(r, 1), core, :, columns], 6, 7),
        ):
            pltpu.make_async_copy(src, weights.at[r, x, c, core, low:high], load_sem.at[r]).start()

    def remote(src, dst, send, recv, device):
        return pltpu.make_async_remote_copy(
            src_ref=src, dst_ref=dst, send_sem=send, recv_sem=recv, device_id=device, device_id_type=MESH
        )

    def wait_load(r):
        ref = weights.at[r, x, c, core]
        pltpu.make_async_copy(ref, ref, load_sem.at[r]).wait()

    def start_plane(r):
        wait_load(r)

        def step(j, carry):
            ref = weights.at[r, x, c, core]
            remote(ref, ref, plane_send.at[r], plane_recv.at[r], (m, lax.rem(c + j, 16))).start()
            return carry
        lax.fori_loop(1, 16, step, 0)

    def plane_bytes(r, sem):
        ref = weights.at[r, x, 0:15, core]
        return pltpu.make_async_copy(ref, ref, sem.at[r])

    def line_copy(r, part, k):
        low, high = PARTS[part]
        ref = weights.at[r, x, :, core, low:high]
        return remote(ref, ref, line_send.at[r, part, k - 1], line_recv.at[r, part, k - 1], line(k))

    def side_copy(r, part, k):
        low, high = PARTS[part]
        ref = weights.at[r, along(-k), :, core, low:high]
        return remote(ref, ref, side_send.at[r, part, k], side_recv.at[r, part, k], sibling)

    def start_line(r):
        plane_bytes(r, plane_recv).wait()
        for part in range(2):
            for k in ORDER:
                line_copy(r, part, k).start()
            side_copy(r, part, 0).start()

    def start_side(r, part):
        for k in ORDER:
            line_copy(r, part, k).wait_recv()
            side_copy(r, part, k).start()

    def wait_side(r, part):
        for k in range(4):
            side_copy(r, part, k).wait_recv()

    def matrix(r, i):
        return jnp.concatenate([weights[r, b, :, :, i].reshape(WIDTH, 128) for b in range(4)], axis=1)

    def slot_copy(k):
        src = own_slots.at[pl.ds(pl.multiple_of(along(k) * PLANE, PLANE), PLANE)]
        return remote(src, line_slots.at[k], slot_send.at[k - 1], slot_recv.at[k - 1], line(k))

    def node_copy(r, k):
        src = node_ref if r == 0 else node_mid
        return remote(src, line_nodes.at[r, k - 1], node_send.at[r, k - 1], node_recv.at[r, k - 1], line(k))

    sub = lax.broadcasted_iota(jnp.int32, (128, 128), 0)
    lane = lax.broadcasted_iota(jnp.int32, (128, 128), 1)
    lane_f = lane.astype(F32)
    at_slot = lane == lax.rem(sub, SLOT)

    def make_pick(k):
        def step(b, carry):
            which = lax.broadcasted_iota(jnp.int32, (128, PLANE), 1)
            row = lax.broadcasted_iota(jnp.int32, (128, PLANE), 0)
            spread = mm(hot(which == 8 * b + row // SLOT), line_slots[k])
            index = jnp.sum(jnp.where(at_slot, spread, 0.0), axis=1, keepdims=True)
            pick_send[k, pl.ds(pl.multiple_of(b * 128, 128), 128), :] = hot(index == lane_f)
            return carry
        lax.fori_loop(0, 4, step, 0)

    def gather(r, k):
        if k:
            nodes = line_nodes[r, k - 1]
        else:
            nodes = node_ref[...] if r == 0 else node_mid[...]
        outgoing[k] = mm(pick_send[k], nodes).astype(BF16)

    def landing(r, k):
        at = ((along(-k) * 2 + core) * 16 + c) * SLOT
        return table.at[r, pl.ds(pl.multiple_of(at, SLOT), SLOT)]

    def send(r, k):
        def step(j, carry):
            q, device = peer(j)
            src = outgoing.at[k, pl.ds(pl.multiple_of(q * SLOT, SLOT), SLOT)]
            remote(src, landing(r, k), ex_send.at[r, k], ex_recv.at[r, k], device).start()
            return carry
        lax.fori_loop(1, PLANE, step, 0)
        if k:
            landing(r, k)[...] = outgoing[k, pl.ds(pl.multiple_of(own * SLOT, SLOT), SLOT), :]
        else:
            landing(r, k)[...] = jnp.zeros((SLOT, WIDTH), BF16)

    def exchange_bytes(sem):
        ref = outgoing.at[0, pl.ds(0, (PLANE - 1) * SLOT)]
        return pltpu.make_async_copy(ref, ref, sem)

    slots = jnp.concatenate([slots_ref[...].astype(F32), jnp.zeros((128 - SLOT, 128), F32)], axis=0)
    own_slots[...] = jnp.transpose(slots).astype(BF16)
    line_slots[0] = own_slots[pl.ds(pl.multiple_of(x * PLANE, PLANE), PLANE), :]
    make_pick(0)
    gather(0, 0)

    pl.semaphore_wait(barrier, 34)
    for k in ORDER:
        slot_copy(k).start()
        node_copy(0, k).start()
    start_plane(0)
    send(0, 0)

    eye = sub == lane
    ones = jnp.ones((128, 128), BF16)

    def column(row):
        wide = jnp.broadcast_to(row.astype(F32), (128, 128))
        return mm(jnp.where(eye, wide, 0.0).astype(BF16), ones)

    def edge_block(i, carry):
        rows = pl.ds(pl.multiple_of(i * 128, 128), 128)
        sender = sender_ref[pl.ds(i, 1), :]
        receiver = receiver_ref[pl.ds(i, 1), :]
        index = column(lax.shift_right_logical(sender, 7)) * 128.0 + column(sender & 127)
        pick_local[rows, :] = hot(index == lane_f)
        for j in range(16):
            pick_sender[j // 4, rows, (j % 4) * 128:(j % 4 + 1) * 128] = hot(index == lane_f + 128.0 * (j + 1))
        pick_receiver[rows, :] = hot(column(receiver) == lane_f)
        sum_receiver[:, rows] = hot(receiver == sub)
        return carry

    def relay(r, k):
        if r == 0:
            slot_copy(k).wait_recv()
            make_pick(k)
        node_copy(r, k).wait_recv()
        gather(r, k)
        send(r, k)

    for k in ORDER[:2]:
        relay(0, k)
    start_line(0)
    relay(0, 2)
    start_plane(1)
    lax.fori_loop(0, EDGE // 128, edge_block, 0)
    start_side(0, 0)

    for r in range(2):
        nodes = node_ref if r == 0 else node_mid
        edges = edge_ref if r == 0 else edge_out_ref
        wait_side(r, 0)
        recv_proj = mm(nodes[...], matrix(r, 2)).astype(BF16)

        def before(t, carry):
            rows = pl.ds(pl.multiple_of(t * TILE, TILE), TILE)
            base[rows, :] = mm(edges[rows, :], matrix(r, 0)) + mm(pick_receiver[rows, :], recv_proj)
            gathered[rows, :] = mm(pick_local[rows, :], nodes[...])
            return carry

        lax.fori_loop(0, EDGE // TILE, before, 0)
        start_side(r, 1)
        for k in (0,) + ORDER:
            exchange_bytes(ex_recv.at[r, k]).wait()
            source = along(-k)

            def arrive(t, carry):
                rows = pl.ds(pl.multiple_of(t * TILE, TILE), TILE)
                block = table[r, pl.ds(pl.multiple_of(source * PLANE_ROWS, PLANE_ROWS), PLANE_ROWS), :]
                gathered[rows, :] += mm(pick_sender[source, rows, :], block)
                return carry

            lax.fori_loop(0, EDGE // TILE, arrive, 0)
        if r == 0:
            start_line(1)

        def after(t, carry):
            rows = pl.ds(pl.multiple_of(t * TILE, TILE), TILE)
            preact = base[rows, :] + mm(gathered[rows, :].astype(BF16), matrix(r, 1))
            output = mm(silu(preact).astype(BF16), matrix(r, 3))
            edge_out_ref[rows, :] = (edges[rows, :].astype(F32) + norm_rows(output)).astype(BF16)
            return carry

        lax.fori_loop(0, EDGE // TILE, after, 0)
        wait_side(r, 1)
        total = mm(sum_receiver[...], edge_out_ref[...]).astype(BF16)
        preact = mm(nodes[...], matrix(r, 4)) + mm(total, matrix(r, 5))
        output = mm(silu(preact).astype(BF16), matrix(r, 6))
        result = (nodes[...].astype(F32) + norm_rows(output)).astype(BF16)
        for k in range(4):
            exchange_bytes(ex_send.at[r, k]).wait()
        if r == 0:
            node_mid[...] = result
            for k in ORDER:
                node_copy(1, k).start()
            gather(1, 0)
            send(1, 0)
            for k in ORDER:
                relay(1, k)
            start_side(1, 0)
        else:
            node_out_ref[...] = result

    for r in range(2):
        plane_bytes(r, plane_send).wait()
        for k in ORDER:
            node_copy(r, k).wait_send()
        for part in range(2):
            for k in ORDER:
                line_copy(r, part, k).wait_send()
            for k in range(4):
                side_copy(r, part, k).wait_send()
    for k in ORDER:
        slot_copy(k).wait_send()


def local(node_latents, edge_latents, sender_slot, receiver_node, send_rows, edge_in, edge_out, node_in, node_out):
    vmem = pl.BlockSpec(memory_space=pltpu.VMEM)
    anywhere = pl.BlockSpec(memory_space=pl.ANY)
    dma = pltpu.SemaphoreType.DMA
    return pl.pallas_call(
        kernel,
        out_shape=(
            jax.ShapeDtypeStruct((NODE, WIDTH), BF16),
            jax.ShapeDtypeStruct((EDGE, WIDTH), BF16),
        ),
        in_specs=[vmem] * 5 + [anywhere] * 4,
        out_specs=(vmem, vmem),
        scratch_shapes=[
            pltpu.VMEM((2, 4, 16, 2, 7, 16, 128), BF16),
            pltpu.VMEM((4, PLANE_ROWS, WIDTH), BF16),
            pltpu.VMEM((2, 4 * PLANE_ROWS, WIDTH), BF16),
            pltpu.VMEM((NODE, WIDTH), BF16),
            pltpu.VMEM((2, 3, NODE, WIDTH), BF16),
            pltpu.VMEM((128, 128), BF16),
            pltpu.VMEM((4, PLANE, 128), BF16),
            pltpu.VMEM((EDGE, NODE), BF16),
            pltpu.VMEM((4, EDGE, PLANE_ROWS), BF16),
            pltpu.VMEM((EDGE, NODE), BF16),
            pltpu.VMEM((NODE, EDGE), BF16),
            pltpu.VMEM((4, PLANE_ROWS, NODE), BF16),
            pltpu.VMEM((EDGE, WIDTH), F32),
            pltpu.VMEM((EDGE, WIDTH), F32),
            dma((2,)), dma((2, 4)), dma((2, 4)), dma((2, 3)), dma((2, 3)), dma((3,)), dma((3,)),
            dma((2,)), dma((2,)), dma((2, 2, 3)), dma((2, 2, 3)), dma((2, 2, 4)), dma((2, 2, 4)),
        ],
        compiler_params=pltpu.CompilerParams(
            collective_id=0, has_side_effects=True, vmem_limit_bytes=56 * 1024 * 1024
        ),
    )(
        node_latents,
        edge_latents,
        sender_slot.reshape(8, 128),
        receiver_node.reshape(8, 128),
        jnp.transpose(send_rows),
        edge_in.reshape(2, 3, 2, 16, WIDTH),
        edge_out.reshape(2, 2, 16, WIDTH),
        node_in.reshape(2, 2, 2, 16, WIDTH),
        node_out.reshape(2, 2, 16, WIDTH),
    )


def solution(mesh):
    rows = P(("mesh", "chan"), None)
    flat = P(("mesh", "chan"))
    return jax.shard_map(
        local,
        mesh=mesh,
        in_specs=(
            rows, rows, flat, flat, rows,
            P(None, None, "chan", None), P(None, "chan", None),
            P(None, None, "chan", None), P(None, "chan", None),
        ),
        out_specs=(rows, rows),
        check_vma=False,
    )
```

```python
import jax
import jax.numpy as jnp
from jax import lax
from jax.experimental import pallas as pl
from jax.experimental.pallas import tpu as pltpu
from jax.sharding import PartitionSpec as P

MESH = pl.DeviceIdType.MESH
F32 = jnp.float32
BF16 = jnp.bfloat16
WIDTH = 512
NODE = 128
EDGE = 1024
SLOT = 16
PLANE = 32
PLANE_ROWS = PLANE * SLOT
TILE = 512
PARTS = ((0, 4), (4, 7))
ORDER = (1, 3, 2)


def mm(a, b):
    return jnp.dot(a, b, preferred_element_type=F32)


def hot(mask):
    return jnp.where(mask, 1.0, 0.0).astype(BF16)


def norm_rows(v):
    mean = jnp.sum(v, axis=1, keepdims=True) * (1.0 / WIDTH)
    square = jnp.sum(v * v, axis=1, keepdims=True) * (1.0 / WIDTH)
    return (v - mean) * lax.rsqrt(square - mean * mean + 1e-05)


def silu(v):
    return v / (1.0 + jnp.exp(-v))


def kernel(
    node_ref, edge_ref, sender_ref, receiver_ref, slots_ref, ein, eout, nin, nout,
    node_out_ref, edge_out_ref,
    weights, outgoing, table, node_mid, line_nodes, own_slots, line_slots,
    pick_local, pick_sender, pick_receiver, sum_receiver, pick_send, base, gathered,
    load_sem, ex_send, ex_recv, node_send, node_recv, slot_send, slot_recv,
    plane_send, plane_recv, line_send, line_recv, half_send, half_recv, side_send, side_recv,
):
    m = lax.axis_index("mesh")
    c = lax.axis_index("chan")
    x, core = m // 2, lax.rem(m, 2)
    own = core * 16 + c
    sibling = (x * 2 + 1 - core, c)

    def along(k):
        return lax.rem(x + k + 4, 4)

    def line(k):
        return (along(k) * 2 + core, c)

    def peer(j):
        q = lax.rem(own + j, PLANE)
        return q, (x * 2 + q // 16, lax.rem(q, 16))

    barrier = pltpu.get_barrier_semaphore()
    for k in ORDER:
        pl.semaphore_signal(barrier, inc=1, device_id=line(k), device_id_type=MESH)

    def greet(j, carry):
        pl.semaphore_signal(barrier, inc=1, device_id=peer(j)[1], device_id_type=MESH)
        return carry

    lax.fori_loop(1, PLANE, greet, 0)

    columns = pl.ds(pl.multiple_of(x * 128, 128), 128)
    for r in range(2):
        for src, low, high in (
            (ein.at[r, :, core, :, columns], 0, 3),
            (eout.at[pl.ds(r, 1), core, :, columns], 3, 4),
            (nin.at[r, :, core, :, columns], 4, 6),
            (nout.at[pl.ds(r, 1), core, :, columns], 6, 7),
        ):
            pltpu.make_async_copy(src, weights.at[r, x, c, core, low:high], load_sem.at[r]).start()

    def remote(src, dst, send, recv, device):
        return pltpu.make_async_remote_copy(
            src_ref=src, dst_ref=dst, send_sem=send, recv_sem=recv, device_id=device, device_id_type=MESH
        )

    def wait_load(r):
        ref = weights.at[r, x, c, core]
        pltpu.make_async_copy(ref, ref, load_sem.at[r]).wait()

    def start_plane(r):
        wait_load(r)

        def step(j, carry):
            ref = weights.at[r, x, c, core]
            remote(ref, ref, plane_send.at[r], plane_recv.at[r], (m, lax.rem(c + j, 16))).start()
            return carry
        lax.fori_loop(1, 16, step, 0)

    def plane_bytes(r, sem):
        ref = weights.at[r, x, 0:15, core]
        return pltpu.make_async_copy(ref, ref, sem.at[r])

    def line_copy(r, part, k):
        low, high = PARTS[part]
        ref = weights.at[r, x, :, core, low:high]
        return remote(ref, ref, line_send.at[r, part, k - 1], line_recv.at[r, part, k - 1], line(k))

    def half_copy(r, part, k):
        low, high = PARTS[part]
        half = pl.ds(0, 8) if k == 1 else pl.ds(8, 8)
        ref = weights.at[r, along(-k), half, core, low:high]
        return remote(ref, ref, half_send.at[r, part, k - 1], half_recv.at[r, part, k - 1], line(k))

    def side_copy(r, part, k):
        low, high = PARTS[part]
        ref = weights.at[r, along(-k), :, core, low:high]
        return remote(ref, ref, side_send.at[r, part, k], side_recv.at[r, part, k], sibling)

    def start_line(r):
        plane_bytes(r, plane_recv).wait()
        for part in range(2):
            for k in (1, 3):
                line_copy(r, part, k).start()
        for part in range(2):
            side_copy(r, part, 0).start()

    def pass_on(r, part):
        for k in (1, 3):
            line_copy(r, part, k).wait_recv()
            half_copy(r, part, k).start()
            side_copy(r, part, k).start()

    def finish_line(r, part):
        for k in (1, 3):
            half_copy(r, part, k).wait_recv()
        side_copy(r, part, 2).start()

    def wait_side(r, part):
        for k in range(4):
            side_copy(r, part, k).wait_recv()

    def matrix(r, i):
        return jnp.concatenate([weights[r, b, :, :, i].reshape(WIDTH, 128) for b in range(4)], axis=1)

    def slot_copy(k):
        src = own_slots.at[pl.ds(pl.multiple_of(along(k) * PLANE, PLANE), PLANE)]
        return remote(src, line_slots.at[k], slot_send.at[k - 1], slot_recv.at[k - 1], line(k))

    def node_copy(r, k):
        src = node_ref if r == 0 else node_mid
        return remote(src, line_nodes.at[r, k - 1], node_send.at[r, k - 1], node_recv.at[r, k - 1], line(k))

    sub = lax.broadcasted_iota(jnp.int32, (128, 128), 0)
    lane = lax.broadcasted_iota(jnp.int32, (128, 128), 1)
    lane_f = lane.astype(F32)
    at_slot = lane == lax.rem(sub, SLOT)

    def make_pick(k):
        def step(b, carry):
            which = lax.broadcasted_iota(jnp.int32, (128, PLANE), 1)
            row = lax.broadcasted_iota(jnp.int32, (128, PLANE), 0)
            spread = mm(hot(which == 8 * b + row // SLOT), line_slots[k])
            index = jnp.sum(jnp.where(at_slot, spread, 0.0), axis=1, keepdims=True)
            pick_send[k, pl.ds(pl.multiple_of(b * 128, 128), 128), :] = hot(index == lane_f)
            return carry
        lax.fori_loop(0, 4, step, 0)

    def gather(r, k):
        if k:
            nodes = line_nodes[r, k - 1]
        else:
            nodes = node_ref[...] if r == 0 else node_mid[...]
        outgoing[k] = mm(pick_send[k], nodes).astype(BF16)

    def landing(r, k):
        at = ((along(-k) * 2 + core) * 16 + c) * SLOT
        return table.at[r, pl.ds(pl.multiple_of(at, SLOT), SLOT)]

    def send(r, k):
        def step(j, carry):
            q, device = peer(j)
            src = outgoing.at[k, pl.ds(pl.multiple_of(q * SLOT, SLOT), SLOT)]
            remote(src, landing(r, k), ex_send.at[r, k], ex_recv.at[r, k], device).start()
            return carry
        lax.fori_loop(1, PLANE, step, 0)
        if k:
            landing(r, k)[...] = outgoing[k, pl.ds(pl.multiple_of(own * SLOT, SLOT), SLOT), :]
        else:
            landing(r, k)[...] = jnp.zeros((SLOT, WIDTH), BF16)

    def exchange_bytes(sem):
        ref = outgoing.at[0, pl.ds(0, (PLANE - 1) * SLOT)]
        return pltpu.make_async_copy(ref, ref, sem)

    slots = jnp.concatenate([slots_ref[...].astype(F32), jnp.zeros((128 - SLOT, 128), F32)], axis=0)
    own_slots[...] = jnp.transpose(slots).astype(BF16)
    line_slots[0] = own_slots[pl.ds(pl.multiple_of(x * PLANE, PLANE), PLANE), :]
    make_pick(0)
    gather(0, 0)

    pl.semaphore_wait(barrier, 34)
    for k in ORDER:
        slot_copy(k).start()
        node_copy(0, k).start()
    start_plane(0)
    send(0, 0)

    eye = sub == lane
    ones = jnp.ones((128, 128), BF16)

    def column(row):
        wide = jnp.broadcast_to(row.astype(F32), (128, 128))
        return mm(jnp.where(eye, wide, 0.0).astype(BF16), ones)

    def edge_block(i, carry):
        rows = pl.ds(pl.multiple_of(i * 128, 128), 128)
        sender = sender_ref[pl.ds(i, 1), :]
        receiver = receiver_ref[pl.ds(i, 1), :]
        index = column(lax.shift_right_logical(sender, 7)) * 128.0 + column(sender & 127)
        pick_local[rows, :] = hot(index == lane_f)
        for j in range(16):
            pick_sender[j // 4, rows, (j % 4) * 128:(j % 4 + 1) * 128] = hot(index == lane_f + 128.0 * (j + 1))
        pick_receiver[rows, :] = hot(column(receiver) == lane_f)
        sum_receiver[:, rows] = hot(receiver == sub)
        return carry

    def relay(r, k):
        if r == 0:
            slot_copy(k).wait_recv()
            make_pick(k)
        node_copy(r, k).wait_recv()
        gather(r, k)
        send(r, k)

    start_plane(1)
    start_line(0)
    relay(0, 1)
    relay(0, 3)
    pass_on(0, 0)
    relay(0, 2)
    pass_on(0, 1)
    finish_line(0, 0)
    lax.fori_loop(0, EDGE // 128, edge_block, 0)
    finish_line(0, 1)
    start_line(1)

    for r in range(2):
        nodes = node_ref if r == 0 else node_mid
        edges = edge_ref if r == 0 else edge_out_ref
        wait_side(r, 0)
        recv_proj = mm(nodes[...], matrix(r, 2)).astype(BF16)

        def before(t, carry):
            rows = pl.ds(pl.multiple_of(t * TILE, TILE), TILE)
            base[rows, :] = mm(edges[rows, :], matrix(r, 0)) + mm(pick_receiver[rows, :], recv_proj)
            gathered[rows, :] = mm(pick_local[rows, :], nodes[...])
            return carry

        lax.fori_loop(0, EDGE // TILE, before, 0)
        for k in (0,) + ORDER:
            exchange_bytes(ex_recv.at[r, k]).wait()
            source = along(-k)

            def arrive(t, carry):
                rows = pl.ds(pl.multiple_of(t * TILE, TILE), TILE)
                block = table[r, pl.ds(pl.multiple_of(source * PLANE_ROWS, PLANE_ROWS), PLANE_ROWS), :]
                gathered[rows, :] += mm(pick_sender[source, rows, :], block)
                return carry

            lax.fori_loop(0, EDGE // TILE, arrive, 0)
        if r == 0:
            pass_on(1, 0)

        def after(t, carry):
            rows = pl.ds(pl.multiple_of(t * TILE, TILE), TILE)
            preact = base[rows, :] + mm(gathered[rows, :].astype(BF16), matrix(r, 1))
            output = mm(silu(preact).astype(BF16), matrix(r, 3))
            edge_out_ref[rows, :] = (edges[rows, :].astype(F32) + norm_rows(output)).astype(BF16)
            return carry

        lax.fori_loop(0, EDGE // TILE, after, 0)
        wait_side(r, 1)
        total = mm(sum_receiver[...], edge_out_ref[...]).astype(BF16)
        preact = mm(nodes[...], matrix(r, 4)) + mm(total, matrix(r, 5))
        output = mm(silu(preact).astype(BF16), matrix(r, 6))
        result = (nodes[...].astype(F32) + norm_rows(output)).astype(BF16)
        for k in range(4):
            exchange_bytes(ex_send.at[r, k]).wait()
        if r == 0:
            node_mid[...] = result
            for k in ORDER:
                node_copy(1, k).start()
            gather(1, 0)
            send(1, 0)
            for k in ORDER:
                relay(1, k)
            finish_line(1, 0)
            pass_on(1, 1)
            finish_line(1, 1)
        else:
            node_out_ref[...] = result

    for r in range(2):
        plane_bytes(r, plane_send).wait()
        for k in ORDER:
            node_copy(r, k).wait_send()
        for part in range(2):
            for k in (1, 3):
                line_copy(r, part, k).wait_send()
                half_copy(r, part, k).wait_send()
            for k in range(4):
                side_copy(r, part, k).wait_send()
    for k in ORDER:
        slot_copy(k).wait_send()


def local(node_latents, edge_latents, sender_slot, receiver_node, send_rows, edge_in, edge_out, node_in, node_out):
    vmem = pl.BlockSpec(memory_space=pltpu.VMEM)
    anywhere = pl.BlockSpec(memory_space=pl.ANY)
    dma = pltpu.SemaphoreType.DMA
    return pl.pallas_call(
        kernel,
        out_shape=(
            jax.ShapeDtypeStruct((NODE, WIDTH), BF16),
            jax.ShapeDtypeStruct((EDGE, WIDTH), BF16),
        ),
        in_specs=[vmem] * 5 + [anywhere] * 4,
        out_specs=(vmem, vmem),
        scratch_shapes=[
            pltpu.VMEM((2, 4, 16, 2, 7, 16, 128), BF16),
            pltpu.VMEM((4, PLANE_ROWS, WIDTH), BF16),
            pltpu.VMEM((2, 4 * PLANE_ROWS, WIDTH), BF16),
            pltpu.VMEM((NODE, WIDTH), BF16),
            pltpu.VMEM((2, 3, NODE, WIDTH), BF16),
            pltpu.VMEM((128, 128), BF16),
            pltpu.VMEM((4, PLANE, 128), BF16),
            pltpu.VMEM((EDGE, NODE), BF16),
            pltpu.VMEM((4, EDGE, PLANE_ROWS), BF16),
            pltpu.VMEM((EDGE, NODE), BF16),
            pltpu.VMEM((NODE, EDGE), BF16),
            pltpu.VMEM((4, PLANE_ROWS, NODE), BF16),
            pltpu.VMEM((EDGE, WIDTH), F32),
            pltpu.VMEM((EDGE, WIDTH), F32),
            dma((2,)), dma((2, 4)), dma((2, 4)), dma((2, 3)), dma((2, 3)), dma((3,)), dma((3,)),
            dma((2,)), dma((2,)), dma((2, 2, 3)), dma((2, 2, 3)), dma((2, 2, 3)), dma((2, 2, 3)), dma((2, 2, 4)), dma((2, 2, 4)),
        ],
        compiler_params=pltpu.CompilerParams(
            collective_id=0, has_side_effects=True, vmem_limit_bytes=56 * 1024 * 1024
        ),
    )(
        node_latents,
        edge_latents,
        sender_slot.reshape(8, 128),
        receiver_node.reshape(8, 128),
        jnp.transpose(send_rows),
        edge_in.reshape(2, 3, 2, 16, WIDTH),
        edge_out.reshape(2, 2, 16, WIDTH),
        node_in.reshape(2, 2, 2, 16, WIDTH),
        node_out.reshape(2, 2, 16, WIDTH),
    )


def solution(mesh):
    rows = P(("mesh", "chan"), None)
    flat = P(("mesh", "chan"))
    return jax.shard_map(
        local,
        mesh=mesh,
        in_specs=(
            rows, rows, flat, flat, rows,
            P(None, None, "chan", None), P(None, "chan", None),
            P(None, None, "chan", None), P(None, "chan", None),
        ),
        out_specs=(rows, rows),
        check_vma=False,
    )
```

```python
import jax
import jax.numpy as jnp
from jax import lax
from jax.experimental import pallas as pl
from jax.experimental.pallas import tpu as pltpu
from jax.sharding import PartitionSpec as P

MESH = pl.DeviceIdType.MESH
F32 = jnp.float32
BF16 = jnp.bfloat16
WIDTH = 512
NODE = 128
EDGE = 1024
SLOT = 16
PLANE = 32
PLANE_ROWS = PLANE * SLOT
TILE = 512
PARTS = ((0, 4), (4, 7))
ORDER = (1, 3, 2)


def mm(a, b):
    return jnp.dot(a, b, preferred_element_type=F32)


def hot(mask):
    return jnp.where(mask, 1.0, 0.0).astype(BF16)


def norm_rows(v):
    mean = jnp.sum(v, axis=1, keepdims=True) * (1.0 / WIDTH)
    square = jnp.sum(v * v, axis=1, keepdims=True) * (1.0 / WIDTH)
    return (v - mean) * lax.rsqrt(square - mean * mean + 1e-05)


def silu(v):
    return v / (1.0 + jnp.exp(-v))


def kernel(
    node_ref, edge_ref, sender_ref, receiver_ref, slots_ref, ein, eout, nin, nout,
    node_out_ref, edge_out_ref,
    weights, outgoing, table, node_mid, line_nodes, own_slots, line_slots,
    pick_local, pick_sender, pick_receiver, sum_receiver, pick_send, base, gathered,
    edges, ready, edge_sem, load_sem, ex_send, ex_recv, node_send, node_recv, slot_send, slot_recv,
    plane_send, plane_recv, line_send, line_recv, half_send, half_recv, side_send, side_recv,
):
    m = lax.axis_index("mesh")
    c = lax.axis_index("chan")
    x, core = m // 2, lax.rem(m, 2)
    own = core * 16 + c
    sibling = (x * 2 + 1 - core, c)

    def along(k):
        return lax.rem(x + k + 4, 4)

    def line(k):
        return (along(k) * 2 + core, c)

    def peer(j):
        q = lax.rem(own + j, PLANE)
        return q, (x * 2 + q // 16, lax.rem(q, 16))

    barrier = pltpu.get_barrier_semaphore()
    for k in ORDER:
        pl.semaphore_signal(barrier, inc=1, device_id=line(k), device_id_type=MESH)

    pl.semaphore_signal(barrier, inc=1, device_id=sibling, device_id_type=MESH)

    def greet(j, carry):
        pl.semaphore_signal(barrier, inc=1, device_id=(m, lax.rem(c + j, 16)), device_id_type=MESH)
        return carry

    lax.fori_loop(1, 16, greet, 0)
    pltpu.make_async_copy(edge_ref, edges, edge_sem.at[0]).start()

    columns = pl.ds(pl.multiple_of(x * 128, 128), 128)
    for r in range(2):
        for src, low, high in (
            (ein.at[r, :, core, :, columns], 0, 3),
            (eout.at[pl.ds(r, 1), core, :, columns], 3, 4),
            (nin.at[r, :, core, :, columns], 4, 6),
            (nout.at[pl.ds(r, 1), core, :, columns], 6, 7),
        ):
            pltpu.make_async_copy(src, weights.at[r, x, c, core, low:high], load_sem.at[r]).start()

    def remote(src, dst, send, recv, device):
        return pltpu.make_async_remote_copy(
            src_ref=src, dst_ref=dst, send_sem=send, recv_sem=recv, device_id=device, device_id_type=MESH
        )

    def wait_load(r):
        ref = weights.at[r, x, c, core]
        pltpu.make_async_copy(ref, ref, load_sem.at[r]).wait()

    def start_plane(r):
        wait_load(r)

        def step(j, carry):
            ref = weights.at[r, x, c, core]
            remote(ref, ref, plane_send.at[r], plane_recv.at[r], (m, lax.rem(c + j, 16))).start()
            return carry
        lax.fori_loop(1, 16, step, 0)

    def plane_bytes(r, sem):
        ref = weights.at[r, x, 0:15, core]
        return pltpu.make_async_copy(ref, ref, sem.at[r])

    def line_copy(r, part, k):
        low, high = PARTS[part]
        ref = weights.at[r, x, :, core, low:high]
        return remote(ref, ref, line_send.at[r, part, k - 1], line_recv.at[r, part, k - 1], line(k))

    def half_copy(r, part, k):
        low, high = PARTS[part]
        half = pl.ds(0, 8) if k == 1 else pl.ds(8, 8)
        ref = weights.at[r, along(-k), half, core, low:high]
        return remote(ref, ref, half_send.at[r, part, k - 1], half_recv.at[r, part, k - 1], line(k))

    def side_copy(r, part, k):
        low, high = PARTS[part]
        ref = weights.at[r, along(-k), :, core, low:high]
        return remote(ref, ref, side_send.at[r, part, k], side_recv.at[r, part, k], sibling)

    def start_line(r):
        plane_bytes(r, plane_recv).wait()
        for part in range(2):
            for k in (1, 3):
                line_copy(r, part, k).start()
        for part in range(2):
            side_copy(r, part, 0).start()

    def pass_on(r, part):
        for k in (1, 3):
            line_copy(r, part, k).wait_recv()
            half_copy(r, part, k).start()
            side_copy(r, part, k).start()

    def finish_line(r, part):
        for k in (1, 3):
            half_copy(r, part, k).wait_recv()
        side_copy(r, part, 2).start()

    def wait_side(r, part):
        for k in range(4):
            side_copy(r, part, k).wait_recv()

    def matrix(r, i):
        return jnp.concatenate([weights[r, b, :, :, i].reshape(WIDTH, 128) for b in range(4)], axis=1)

    def slot_copy(k):
        src = own_slots.at[pl.ds(pl.multiple_of(along(k) * PLANE, PLANE), PLANE)]
        return remote(src, line_slots.at[k], slot_send.at[k - 1], slot_recv.at[k - 1], line(k))

    def node_copy(r, k):
        src = node_ref if r == 0 else node_mid
        return remote(src, line_nodes.at[r, k - 1], node_send.at[r, k - 1], node_recv.at[r, k - 1], line(k))

    sub = lax.broadcasted_iota(jnp.int32, (128, 128), 0)
    lane = lax.broadcasted_iota(jnp.int32, (128, 128), 1)
    lane_f = lane.astype(F32)
    at_slot = lane == lax.rem(sub, SLOT)

    def make_pick(k):
        def step(b, carry):
            which = lax.broadcasted_iota(jnp.int32, (128, PLANE), 1)
            row = lax.broadcasted_iota(jnp.int32, (128, PLANE), 0)
            spread = mm(hot(which == 8 * b + row // SLOT), line_slots[k])
            index = jnp.sum(jnp.where(at_slot, spread, 0.0), axis=1, keepdims=True)
            pick_send[k, pl.ds(pl.multiple_of(b * 128, 128), 128), :] = hot(index == lane_f)
            return carry
        lax.fori_loop(0, 4, step, 0)

    def gather(r, k):
        if k:
            nodes = line_nodes[r, k - 1]
        else:
            nodes = node_ref[...] if r == 0 else node_mid[...]
        outgoing[k] = mm(pick_send[k], nodes).astype(BF16)

    def landing(r, k):
        at = ((along(-k) * 2 + core) * 16 + c) * SLOT
        return table.at[r, pl.ds(pl.multiple_of(at, SLOT), SLOT)]

    def send(r, k):
        def step(j, carry):
            q, device = peer(j)
            src = outgoing.at[k, pl.ds(pl.multiple_of(q * SLOT, SLOT), SLOT)]
            remote(src, landing(r, k), ex_send.at[r, k], ex_recv.at[r, k], device).start()
            return carry
        lax.fori_loop(1, PLANE, step, 0)
        if k:
            landing(r, k)[...] = outgoing[k, pl.ds(pl.multiple_of(own * SLOT, SLOT), SLOT), :]
        else:
            landing(r, k)[...] = jnp.zeros((SLOT, WIDTH), BF16)

    def exchange_bytes(sem):
        ref = outgoing.at[0, pl.ds(0, (PLANE - 1) * SLOT)]
        return pltpu.make_async_copy(ref, ref, sem)

    slots = jnp.concatenate([slots_ref[...].astype(F32), jnp.zeros((128 - SLOT, 128), F32)], axis=0)
    own_slots[...] = jnp.transpose(slots).astype(BF16)
    line_slots[0] = own_slots[pl.ds(pl.multiple_of(x * PLANE, PLANE), PLANE), :]
    make_pick(0)
    gather(0, 0)

    pl.semaphore_wait(barrier, 19)
    pl.semaphore_signal(ready, inc=1, device_id=sibling, device_id_type=MESH)
    for k in ORDER:
        slot_copy(k).start()
        node_copy(0, k).start()
    start_plane(0)
    pl.semaphore_wait(ready, 1)
    send(0, 0)

    eye = sub == lane
    ones = jnp.ones((128, 128), BF16)

    def column(row):
        wide = jnp.broadcast_to(row.astype(F32), (128, 128))
        return mm(jnp.where(eye, wide, 0.0).astype(BF16), ones)

    def edge_block(i, carry):
        rows = pl.ds(pl.multiple_of(i * 128, 128), 128)
        sender = sender_ref[pl.ds(i, 1), :]
        receiver = receiver_ref[pl.ds(i, 1), :]
        index = column(lax.shift_right_logical(sender, 7)) * 128.0 + column(sender & 127)
        pick_local[rows, :] = hot(index == lane_f)
        for j in range(16):
            pick_sender[j // 4, rows, (j % 4) * 128:(j % 4 + 1) * 128] = hot(index == lane_f + 128.0 * (j + 1))
        pick_receiver[rows, :] = hot(column(receiver) == lane_f)
        sum_receiver[:, rows] = hot(receiver == sub)
        return carry

    def relay(r, k):
        if r == 0:
            slot_copy(k).wait_recv()
            make_pick(k)
        node_copy(r, k).wait_recv()
        gather(r, k)
        send(r, k)

    def tiles(step):
        def body(t, carry):
            step(pl.ds(pl.multiple_of(t * TILE, TILE), TILE))
            return carry
        lax.fori_loop(0, EDGE // TILE, body, 0)

    def picked(r, k, rows):
        source = along(-k)
        block = table[r, pl.ds(pl.multiple_of(source * PLANE_ROWS, PLANE_ROWS), PLANE_ROWS), :]
        return mm(pick_sender[source, rows, :], block)

    def arrive(r, k):
        nodes = node_ref if r == 0 else node_mid
        exchange_bytes(ex_recv.at[r, k]).wait()

        def step(rows):
            if k == 0:
                gathered[rows, :] = mm(pick_local[rows, :], nodes[...]) + picked(r, k, rows)
            else:
                gathered[rows, :] += picked(r, k, rows)
        tiles(step)

    def before(r):
        nodes = node_ref if r == 0 else node_mid
        wait_side(r, 0)
        recv_proj = mm(nodes[...], matrix(r, 2)).astype(BF16)

        def step(rows):
            base[rows, :] = mm(edges[rows, :], matrix(r, 0)) + mm(pick_receiver[rows, :], recv_proj)
        tiles(step)

    def after(r, k):
        exchange_bytes(ex_recv.at[r, k]).wait()

        def step(rows):
            sender_rows = gathered[rows, :] + picked(r, k, rows)
            preact = base[rows, :] + mm(sender_rows.astype(BF16), matrix(r, 1))
            output = mm(silu(preact).astype(BF16), matrix(r, 3))
            edges[rows, :] = (edges[rows, :].astype(F32) + norm_rows(output)).astype(BF16)
        tiles(step)

    def update(r):
        nodes = node_ref if r == 0 else node_mid
        wait_side(r, 1)
        total = mm(sum_receiver[...], edges[...]).astype(BF16)
        preact = mm(nodes[...], matrix(r, 4)) + mm(total, matrix(r, 5))
        output = mm(silu(preact).astype(BF16), matrix(r, 6))
        return (nodes[...].astype(F32) + norm_rows(output)).astype(BF16)

    lax.fori_loop(0, EDGE // 128, edge_block, 0)
    start_line(0)
    relay(0, 1)
    relay(0, 3)
    pass_on(0, 0)
    relay(0, 2)
    start_plane(1)
    pass_on(0, 1)
    arrive(0, 0)
    finish_line(0, 0)
    finish_line(0, 1)
    arrive(0, 1)
    pltpu.make_async_copy(edge_ref, edges, edge_sem.at[0]).wait()
    before(0)
    arrive(0, 3)
    after(0, 2)
    node_mid[...] = update(0)

    for k in ORDER:
        node_copy(1, k).start()
    for k in range(4):
        exchange_bytes(ex_send.at[0, k]).wait()
    gather(1, 0)
    send(1, 0)
    start_line(1)
    for k in ORDER:
        relay(1, k)
    pass_on(1, 0)
    arrive(1, 0)
    pass_on(1, 1)
    arrive(1, 1)
    finish_line(1, 0)
    arrive(1, 3)
    finish_line(1, 1)
    before(1)
    after(1, 2)
    pltpu.make_async_copy(edges, edge_out_ref, edge_sem.at[1]).start()
    node_out_ref[...] = update(1)

    for k in range(4):
        exchange_bytes(ex_send.at[1, k]).wait()
    pltpu.make_async_copy(edges, edge_out_ref, edge_sem.at[1]).wait()
    for r in range(2):
        plane_bytes(r, plane_send).wait()
        for k in ORDER:
            node_copy(r, k).wait_send()
        for part in range(2):
            for k in (1, 3):
                line_copy(r, part, k).wait_send()
                half_copy(r, part, k).wait_send()
            for k in range(4):
                side_copy(r, part, k).wait_send()
    for k in ORDER:
        slot_copy(k).wait_send()


def local(node_latents, edge_latents, sender_slot, receiver_node, send_rows, edge_in, edge_out, node_in, node_out):
    vmem = pl.BlockSpec(memory_space=pltpu.VMEM)
    anywhere = pl.BlockSpec(memory_space=pl.ANY)
    dma = pltpu.SemaphoreType.DMA
    return pl.pallas_call(
        kernel,
        out_shape=(
            jax.ShapeDtypeStruct((NODE, WIDTH), BF16),
            jax.ShapeDtypeStruct((EDGE, WIDTH), BF16),
        ),
        in_specs=[vmem, anywhere] + [vmem] * 3 + [anywhere] * 4,
        out_specs=(vmem, anywhere),
        scratch_shapes=[
            pltpu.VMEM((2, 4, 16, 2, 7, 16, 128), BF16),
            pltpu.VMEM((4, PLANE_ROWS, WIDTH), BF16),
            pltpu.VMEM((2, 4 * PLANE_ROWS, WIDTH), BF16),
            pltpu.VMEM((NODE, WIDTH), BF16),
            pltpu.VMEM((2, 3, NODE, WIDTH), BF16),
            pltpu.VMEM((128, 128), BF16),
            pltpu.VMEM((4, PLANE, 128), BF16),
            pltpu.VMEM((EDGE, NODE), BF16),
            pltpu.VMEM((4, EDGE, PLANE_ROWS), BF16),
            pltpu.VMEM((EDGE, NODE), BF16),
            pltpu.VMEM((NODE, EDGE), BF16),
            pltpu.VMEM((4, PLANE_ROWS, NODE), BF16),
            pltpu.VMEM((EDGE, WIDTH), F32),
            pltpu.VMEM((EDGE, WIDTH), F32),
            pltpu.VMEM((EDGE, WIDTH), BF16),
            pltpu.SemaphoreType.REGULAR,
            dma((2,)), dma((2,)), dma((2, 4)), dma((2, 4)), dma((2, 3)), dma((2, 3)), dma((3,)), dma((3,)),
            dma((2,)), dma((2,)), dma((2, 2, 3)), dma((2, 2, 3)), dma((2, 2, 3)), dma((2, 2, 3)), dma((2, 2, 4)), dma((2, 2, 4)),
        ],
        compiler_params=pltpu.CompilerParams(
            collective_id=0, has_side_effects=True, vmem_limit_bytes=56 * 1024 * 1024
        ),
    )(
        node_latents,
        edge_latents,
        sender_slot.reshape(8, 128),
        receiver_node.reshape(8, 128),
        jnp.transpose(send_rows),
        edge_in.reshape(2, 3, 2, 16, WIDTH),
        edge_out.reshape(2, 2, 16, WIDTH),
        node_in.reshape(2, 2, 2, 16, WIDTH),
        node_out.reshape(2, 2, 16, WIDTH),
    )


def solution(mesh):
    rows = P(("mesh", "chan"), None)
    flat = P(("mesh", "chan"))
    return jax.shard_map(
        local,
        mesh=mesh,
        in_specs=(
            rows, rows, flat, flat, rows,
            P(None, None, "chan", None), P(None, "chan", None),
            P(None, None, "chan", None), P(None, "chan", None),
        ),
        out_specs=(rows, rows),
        check_vma=False,
    )
```

```python
import jax
import jax.numpy as jnp
from jax import lax
from jax.experimental import pallas as pl
from jax.experimental.pallas import tpu as pltpu
from jax.sharding import PartitionSpec as P

MESH = pl.DeviceIdType.MESH
F32 = jnp.float32
BF16 = jnp.bfloat16
WIDTH = 512
NODE = 128
EDGE = 1024
SLOT = 16
PLANE = 32
PLANE_ROWS = PLANE * SLOT
TILE = 512
PARTS = ((0, 4), (4, 7))
ORDER = (1, 3, 2)


def mm(a, b):
    return jnp.dot(a, b, preferred_element_type=F32)


def hot(mask):
    return jnp.where(mask, 1.0, 0.0).astype(BF16)


def norm_rows(v):
    mean = jnp.sum(v, axis=1, keepdims=True) * (1.0 / WIDTH)
    square = jnp.sum(v * v, axis=1, keepdims=True) * (1.0 / WIDTH)
    return (v - mean) * lax.rsqrt(square - mean * mean + 1e-05)


def silu(v):
    half = 0.5 * v
    return half + half * jnp.tanh(half)


def kernel(
    node_in, edge_ref, sender_in, receiver_in, slots_in, ein, eout, nin, nout,
    node_out_ref, edge_out_ref,
    weights, outgoing, table, node_mid, line_nodes, own_slots, line_slots,
    pick_local, pick_sender, pick_receiver, sum_receiver, pick_send, base, gathered,
    node_ref, sender_ref, receiver_ref, slots_ref, edges, projected, ready, small_sem, edge_sem, load_sem, ex_send, ex_recv, node_send, node_recv, slot_send, slot_recv,
    plane_send, plane_recv, line_send, line_recv, half_send, half_recv, side_send, side_recv,
):
    m = lax.axis_index("mesh")
    c = lax.axis_index("chan")
    x, core = m // 2, lax.rem(m, 2)
    own = core * 16 + c
    sibling = (x * 2 + 1 - core, c)

    def along(k):
        return lax.rem(x + k + 4, 4)

    def line(k):
        return (along(k) * 2 + core, c)

    barrier = pltpu.get_barrier_semaphore()
    for k in ORDER:
        pl.semaphore_signal(barrier, inc=1, device_id=line(k), device_id_type=MESH)

    pl.semaphore_signal(barrier, inc=1, device_id=sibling, device_id_type=MESH)

    def greet(j, carry):
        pl.semaphore_signal(barrier, inc=1, device_id=(m, lax.rem(c + j, 16)), device_id_type=MESH)
        return carry

    lax.fori_loop(1, 16, greet, 0)
    smalls = [
        pltpu.make_async_copy(src, dst, small_sem.at[i])
        for i, (src, dst) in enumerate(
            ((slots_in, slots_ref), (node_in, node_ref), (sender_in, sender_ref), (receiver_in, receiver_ref))
        )
    ]
    for small in smalls:
        small.start()
    pltpu.make_async_copy(edge_ref, edges, edge_sem.at[0]).start()

    columns = pl.ds(pl.multiple_of(x * 128, 128), 128)
    for r in range(2):
        for src, low, high in (
            (ein.at[r, :, core, :, columns], 0, 3),
            (eout.at[pl.ds(r, 1), core, :, columns], 3, 4),
            (nin.at[r, :, core, :, columns], 4, 6),
            (nout.at[pl.ds(r, 1), core, :, columns], 6, 7),
        ):
            pltpu.make_async_copy(src, weights.at[r, x, c, core, low:high], load_sem.at[r]).start()

    def remote(src, dst, send, recv, device):
        return pltpu.make_async_remote_copy(
            src_ref=src, dst_ref=dst, send_sem=send, recv_sem=recv, device_id=device, device_id_type=MESH
        )

    def wait_load(r):
        ref = weights.at[r, x, c, core]
        pltpu.make_async_copy(ref, ref, load_sem.at[r]).wait()

    def start_plane(r):
        wait_load(r)

        def step(j, carry):
            ref = weights.at[r, x, c, core]
            remote(ref, ref, plane_send.at[r], plane_recv.at[r], (m, lax.rem(c + j, 16))).start()
            return carry
        lax.fori_loop(1, 16, step, 0)

    def plane_bytes(r, sem):
        ref = weights.at[r, x, 0:15, core]
        return pltpu.make_async_copy(ref, ref, sem.at[r])

    def line_copy(r, part, k):
        low, high = PARTS[part]
        ref = weights.at[r, x, :, core, low:high]
        return remote(ref, ref, line_send.at[r, part, k - 1], line_recv.at[r, part, k - 1], line(k))

    def half_copy(r, part, k):
        low, high = PARTS[part]
        half = pl.ds(0, 8) if k == 1 else pl.ds(8, 8)
        ref = weights.at[r, along(-k), half, core, low:high]
        return remote(ref, ref, half_send.at[r, part, k - 1], half_recv.at[r, part, k - 1], line(k))

    def side_copy(r, part, k):
        low, high = PARTS[part]
        ref = weights.at[r, along(-k), :, core, low:high]
        return remote(ref, ref, side_send.at[r, part, k], side_recv.at[r, part, k], sibling)

    def start_line(r):
        plane_bytes(r, plane_recv).wait()
        for part in range(2):
            for k in (1, 3):
                line_copy(r, part, k).start()
        for part in range(2):
            side_copy(r, part, 0).start()

    def pass_on(r, part):
        for k in (1, 3):
            line_copy(r, part, k).wait_recv()
            half_copy(r, part, k).start()
            side_copy(r, part, k).start()

    def finish_line(r, part):
        for k in (1, 3):
            half_copy(r, part, k).wait_recv()
        side_copy(r, part, 2).start()

    def wait_side(r, part):
        for k in range(4):
            side_copy(r, part, k).wait_recv()

    def matrix(r, i):
        return jnp.concatenate([weights[r, b, :, :, i].reshape(WIDTH, 128) for b in range(4)], axis=1)

    def slot_copy(k):
        src = own_slots.at[pl.ds(pl.multiple_of(along(k) * PLANE, PLANE), PLANE)]
        return remote(src, line_slots.at[k], slot_send.at[k - 1], slot_recv.at[k - 1], line(k))

    def node_copy(r, k):
        src = node_ref if r == 0 else node_mid
        return remote(src, line_nodes.at[r, k - 1], node_send.at[r, k - 1], node_recv.at[r, k - 1], line(k))

    sub = lax.broadcasted_iota(jnp.int32, (128, 128), 0)
    lane = lax.broadcasted_iota(jnp.int32, (128, 128), 1)
    lane_f = lane.astype(F32)
    at_slot = lane == lax.rem(sub, SLOT)

    def make_pick(k):
        def step(b, carry):
            which = lax.broadcasted_iota(jnp.int32, (128, PLANE), 1)
            row = lax.broadcasted_iota(jnp.int32, (128, PLANE), 0)
            spread = mm(hot(which == 8 * b + row // SLOT), line_slots[k])
            index = jnp.sum(jnp.where(at_slot, spread, 0.0), axis=1, keepdims=True)
            pick_send[k, pl.ds(pl.multiple_of(b * 128, 128), 128), :] = hot(index == lane_f)
            return carry
        lax.fori_loop(0, 4, step, 0)

    def gather(r, k):
        if k:
            nodes = line_nodes[r, k - 1]
        else:
            nodes = node_ref[...] if r == 0 else node_mid[...]
        outgoing[k] = mm(pick_send[k], nodes).astype(BF16)

    def landing(r, k):
        at = ((along(-k) * 2 + core) * 16 + c) * SLOT
        return table.at[r, pl.ds(pl.multiple_of(at, SLOT), SLOT)]

    def send(r, k):
        for side in range(2):
            def step(j, carry):
                chan = lax.rem(c + j, 16)
                to_core = lax.rem(core + side, 2)
                q = to_core * 16 + chan
                src = outgoing.at[k, pl.ds(pl.multiple_of(q * SLOT, SLOT), SLOT)]
                remote(
                    src, landing(r, k), ex_send.at[r, k, side], ex_recv.at[r, k, side], (x * 2 + to_core, chan)
                ).start()
                return carry
            lax.fori_loop(1 - side, 16, step, 0)
        if k:
            landing(r, k)[...] = outgoing[k, pl.ds(pl.multiple_of(own * SLOT, SLOT), SLOT), :]
        else:
            landing(r, k)[...] = jnp.zeros((SLOT, WIDTH), BF16)

    def wait_exchange(sem, r, k, side):
        ref = outgoing.at[0, pl.ds(0, (15 + side) * SLOT)]
        pltpu.make_async_copy(ref, ref, sem.at[r, k, side]).wait()

    for small in smalls:
        small.wait()
    slots = jnp.concatenate([slots_ref[...].astype(F32), jnp.zeros((128 - SLOT, 128), F32)], axis=0)
    own_slots[...] = jnp.transpose(slots).astype(BF16)
    line_slots[0] = own_slots[pl.ds(pl.multiple_of(x * PLANE, PLANE), PLANE), :]
    make_pick(0)
    gather(0, 0)

    pl.semaphore_wait(barrier, 19)
    pl.semaphore_signal(ready, inc=1, device_id=sibling, device_id_type=MESH)
    for k in ORDER:
        slot_copy(k).start()
        node_copy(0, k).start()
    start_plane(0)
    pl.semaphore_wait(ready, 1)
    send(0, 0)

    eye = sub == lane
    ones = jnp.ones((128, 128), BF16)

    def column(row):
        wide = jnp.broadcast_to(row.astype(F32), (128, 128))
        return mm(jnp.where(eye, wide, 0.0).astype(BF16), ones)

    def edge_block(i, carry):
        rows = pl.ds(pl.multiple_of(i * 128, 128), 128)
        sender = sender_ref[pl.ds(i, 1), :]
        receiver = receiver_ref[pl.ds(i, 1), :]
        index = column(lax.shift_right_logical(sender, 7)) * 128.0 + column(sender & 127)
        pick_local[rows, :] = hot(index == lane_f)
        for j in range(16):
            pick_sender[j // 4, rows, (j % 4) * 128:(j % 4 + 1) * 128] = hot(index == lane_f + 128.0 * (j + 1))
        pick_receiver[rows, :] = hot(column(receiver) == lane_f)
        sum_receiver[:, rows] = hot(receiver == sub)
        return carry

    def relay(r, k):
        if r == 0:
            slot_copy(k).wait_recv()
            make_pick(k)
        node_copy(r, k).wait_recv()
        gather(r, k)
        send(r, k)

    def tiles(step):
        for t in range(EDGE // TILE):
            step(slice(t * TILE, (t + 1) * TILE))

    def picked(r, k, rows):
        source = along(-k)
        block = table[r, pl.ds(pl.multiple_of(source * PLANE_ROWS, PLANE_ROWS), PLANE_ROWS), :]
        return mm(pick_sender[source, rows, :], block)

    def arrive(r, k):
        nodes = node_ref if r == 0 else node_mid
        for side in range(2):
            wait_exchange(ex_recv, r, k, side)

        def step(rows):
            if k == 0:
                gathered[rows, :] = mm(pick_local[rows, :], nodes[...]) + picked(r, k, rows)
            else:
                gathered[rows, :] += picked(r, k, rows)
        tiles(step)

    def before(r):
        nodes = node_ref if r == 0 else node_mid
        wait_side(r, 0)
        recv_proj = mm(nodes[...], matrix(r, 2)).astype(BF16)

        def step(rows):
            total = mm(edges[rows, :], matrix(r, 0)) + mm(pick_receiver[rows, :], recv_proj)
            base[rows, :] = total + mm(gathered[rows, :].astype(BF16), matrix(r, 1))
        tiles(step)

    def after(r, k):
        source = along(-k)
        half = PLANE_ROWS // 2
        for side in range(2):
            wait_exchange(ex_recv, r, k, side)
            at = lax.rem(core + side, 2) * half
            block = table[r, pl.ds(pl.multiple_of(source * PLANE_ROWS + at, half), half), :]
            projected[pl.ds(pl.multiple_of(at, half), half), :] = mm(block, matrix(r, 1)).astype(BF16)

        def step(rows):
            preact = base[rows, :] + mm(pick_sender[source, rows, :], projected[...])
            output = mm(silu(preact).astype(BF16), matrix(r, 3))
            edges[rows, :] = (edges[rows, :].astype(F32) + norm_rows(output)).astype(BF16)
        tiles(step)

    def update(r):
        nodes = node_ref if r == 0 else node_mid
        wait_side(r, 1)
        total = mm(sum_receiver[...], edges[...]).astype(BF16)
        preact = mm(nodes[...], matrix(r, 4)) + mm(total, matrix(r, 5))
        output = mm(silu(preact).astype(BF16), matrix(r, 6))
        return (nodes[...].astype(F32) + norm_rows(output)).astype(BF16)

    lax.fori_loop(0, EDGE // 128, edge_block, 0)
    start_line(0)
    relay(0, 1)
    relay(0, 3)
    pass_on(0, 0)
    relay(0, 2)
    start_plane(1)
    pass_on(0, 1)
    arrive(0, 0)
    finish_line(0, 0)
    finish_line(0, 1)
    arrive(0, 1)
    arrive(0, 3)
    pltpu.make_async_copy(edge_ref, edges, edge_sem.at[0]).wait()
    before(0)
    after(0, 2)
    node_mid[...] = update(0)

    for k in ORDER:
        node_copy(1, k).start()
    for k in range(4):
        for side in range(2):
            wait_exchange(ex_send, 0, k, side)
    gather(1, 0)
    send(1, 0)
    start_line(1)
    for k in ORDER:
        relay(1, k)
    pass_on(1, 0)
    arrive(1, 0)
    pass_on(1, 1)
    arrive(1, 1)
    finish_line(1, 0)
    arrive(1, 3)
    finish_line(1, 1)
    before(1)
    after(1, 2)
    pltpu.make_async_copy(edges, edge_out_ref, edge_sem.at[1]).start()
    node_out_ref[...] = update(1)

    for k in range(4):
        for side in range(2):
            wait_exchange(ex_send, 1, k, side)
    pltpu.make_async_copy(edges, edge_out_ref, edge_sem.at[1]).wait()
    for r in range(2):
        plane_bytes(r, plane_send).wait()
        for k in ORDER:
            node_copy(r, k).wait_send()
        for part in range(2):
            for k in (1, 3):
                line_copy(r, part, k).wait_send()
                half_copy(r, part, k).wait_send()
            for k in range(4):
                side_copy(r, part, k).wait_send()
    for k in ORDER:
        slot_copy(k).wait_send()


def hand_out(node_ref, edge_ref, node_out_ref, edge_out_ref, node_buf, edge_buf, sems):
    pieces = [(node_ref, node_buf, node_out_ref)]
    for i in range(4):
        rows = pl.ds(i * (EDGE // 4), EDGE // 4)
        pieces.append((edge_ref.at[rows], edge_buf.at[rows], edge_out_ref.at[rows]))
    loads = [pltpu.make_async_copy(src, buf, sems.at[0, i]) for i, (src, buf, _) in enumerate(pieces)]
    stores = [pltpu.make_async_copy(buf, dst, sems.at[1, i]) for i, (_, buf, dst) in enumerate(pieces)]
    for load in loads:
        load.start()
    for load, store in zip(loads, stores):
        load.wait()
        store.start()
    for store in stores:
        store.wait()


def local(node_latents, edge_latents, sender_slot, receiver_node, send_rows, edge_in, edge_out, node_in, node_out):
    vmem = pl.BlockSpec(memory_space=pltpu.VMEM)
    anywhere = pl.BlockSpec(memory_space=pl.ANY)
    dma = pltpu.SemaphoreType.DMA
    node_state, edge_state = pl.pallas_call(
        kernel,
        out_shape=(
            jax.ShapeDtypeStruct((NODE, WIDTH), BF16),
            jax.ShapeDtypeStruct((EDGE, WIDTH), BF16),
        ),
        in_specs=[anywhere] * 9,
        out_specs=(vmem, anywhere),
        scratch_shapes=[
            pltpu.VMEM((2, 4, 16, 2, 7, 16, 128), BF16),
            pltpu.VMEM((4, PLANE_ROWS, WIDTH), BF16),
            pltpu.VMEM((2, 4 * PLANE_ROWS, WIDTH), BF16),
            pltpu.VMEM((NODE, WIDTH), BF16),
            pltpu.VMEM((2, 3, NODE, WIDTH), BF16),
            pltpu.VMEM((128, 128), BF16),
            pltpu.VMEM((4, PLANE, 128), BF16),
            pltpu.VMEM((EDGE, NODE), BF16),
            pltpu.VMEM((4, EDGE, PLANE_ROWS), BF16),
            pltpu.VMEM((EDGE, NODE), BF16),
            pltpu.VMEM((NODE, EDGE), BF16),
            pltpu.VMEM((4, PLANE_ROWS, NODE), BF16),
            pltpu.VMEM((EDGE, WIDTH), F32),
            pltpu.VMEM((EDGE, WIDTH), F32),
            pltpu.VMEM((NODE, WIDTH), BF16),
            pltpu.VMEM((8, 128), jnp.int32),
            pltpu.VMEM((8, 128), jnp.int32),
            pltpu.VMEM((SLOT, 128), jnp.int32),
            pltpu.VMEM((EDGE, WIDTH), BF16),
            pltpu.VMEM((PLANE_ROWS, WIDTH), BF16),
            pltpu.SemaphoreType.REGULAR,
            dma((4,)),
            dma((2,)), dma((2,)), dma((2, 4, 2)), dma((2, 4, 2)), dma((2, 3)), dma((2, 3)), dma((3,)), dma((3,)),
            dma((2,)), dma((2,)), dma((2, 2, 3)), dma((2, 2, 3)), dma((2, 2, 3)), dma((2, 2, 3)), dma((2, 2, 4)), dma((2, 2, 4)),
        ],
        compiler_params=pltpu.CompilerParams(
            collective_id=0, has_side_effects=True, vmem_limit_bytes=56 * 1024 * 1024
        ),
    )(
        node_latents,
        edge_latents,
        sender_slot.reshape(8, 128),
        receiver_node.reshape(8, 128),
        jnp.transpose(send_rows),
        edge_in.reshape(2, 3, 2, 16, WIDTH),
        edge_out.reshape(2, 2, 16, WIDTH),
        node_in.reshape(2, 2, 2, 16, WIDTH),
        node_out.reshape(2, 2, 16, WIDTH),
    )
    return pl.pallas_call(
        hand_out,
        out_shape=(
            jax.ShapeDtypeStruct((NODE, WIDTH), BF16),
            jax.ShapeDtypeStruct((EDGE, WIDTH), BF16),
        ),
        in_specs=[anywhere] * 2,
        out_specs=(anywhere, anywhere),
        scratch_shapes=[pltpu.VMEM((NODE, WIDTH), BF16), pltpu.VMEM((EDGE, WIDTH), BF16), dma((2, 5))],
    )(node_state, edge_state)


def solution(mesh):
    rows = P(("mesh", "chan"), None)
    flat = P(("mesh", "chan"))
    return jax.shard_map(
        local,
        mesh=mesh,
        in_specs=(
            rows, rows, flat, flat, rows,
            P(None, None, "chan", None), P(None, "chan", None),
            P(None, None, "chan", None), P(None, "chan", None),
        ),
        out_specs=(rows, rows),
        check_vma=False,
    )
```

```python
import jax
import jax.numpy as jnp
from jax import lax
from jax.experimental import pallas as pl
from jax.experimental.pallas import tpu as pltpu
from jax.sharding import PartitionSpec as P

MESH = pl.DeviceIdType.MESH
F32 = jnp.float32
BF16 = jnp.bfloat16
WIDTH = 512
NODE = 128
EDGE = 1024
SLOT = 16
PLANE = 32
PLANE_ROWS = PLANE * SLOT
TILE = 512
PARTS = ((0, 4), (4, 7))
ORDER = (1, 3, 2)


def mm(a, b):
    return jnp.dot(a, b, preferred_element_type=F32)


def hot(mask):
    return jnp.where(mask, 1.0, 0.0).astype(BF16)


def norm_rows(v):
    mean = jnp.sum(v, axis=1, keepdims=True) * (1.0 / WIDTH)
    square = jnp.sum(v * v, axis=1, keepdims=True) * (1.0 / WIDTH)
    return (v - mean) * lax.rsqrt(square - mean * mean + 1e-05)


def silu(v):
    half = 0.5 * v
    return half + half * jnp.tanh(half)


def kernel(
    node_in, edge_ref, sender_in, receiver_in, slots_in, ein, eout, nin, nout,
    node_out_ref, edge_out_ref,
    weights, outgoing, table, node_mid, line_nodes, own_slots, line_slots,
    pick_local, pick_sender, pick_receiver, sum_receiver, pick_send, base, gathered,
    node_ref, sender_ref, receiver_ref, slots_ref, edges, projected, ready, small_sem, edge_sem, load_sem, ex_send, ex_recv, node_send, node_recv, slot_send, slot_recv,
    plane_send, plane_recv, line_send, line_recv, half_send, half_recv, side_send, side_recv,
):
    m = lax.axis_index("mesh")
    c = lax.axis_index("chan")
    x, core = m // 2, lax.rem(m, 2)
    own = core * 16 + c
    sibling = (x * 2 + 1 - core, c)

    def along(k):
        return lax.rem(x + k + 4, 4)

    def line(k):
        return (along(k) * 2 + core, c)

    barrier = pltpu.get_barrier_semaphore()
    for k in ORDER:
        pl.semaphore_signal(barrier, inc=1, device_id=line(k), device_id_type=MESH)

    pl.semaphore_signal(barrier, inc=1, device_id=sibling, device_id_type=MESH)

    def greet(j, carry):
        pl.semaphore_signal(barrier, inc=1, device_id=(m, lax.rem(c + j, 16)), device_id_type=MESH)
        return carry

    lax.fori_loop(1, 16, greet, 0)
    smalls = [
        pltpu.make_async_copy(src, dst, small_sem.at[i])
        for i, (src, dst) in enumerate(
            ((slots_in, slots_ref), (node_in, node_ref), (sender_in, sender_ref), (receiver_in, receiver_ref))
        )
    ]
    for small in smalls:
        small.start()
    pltpu.make_async_copy(edge_ref, edges, edge_sem.at[0]).start()

    columns = pl.ds(pl.multiple_of(x * 128, 128), 128)
    for r in range(2):
        for src, low, high in (
            (ein.at[r, :, core, :, columns], 0, 3),
            (eout.at[pl.ds(r, 1), core, :, columns], 3, 4),
            (nin.at[r, :, core, :, columns], 4, 6),
            (nout.at[pl.ds(r, 1), core, :, columns], 6, 7),
        ):
            pltpu.make_async_copy(src, weights.at[r, x, c, core, low:high], load_sem.at[r]).start()

    def remote(src, dst, send, recv, device):
        return pltpu.make_async_remote_copy(
            src_ref=src, dst_ref=dst, send_sem=send, recv_sem=recv, device_id=device, device_id_type=MESH
        )

    def wait_load(r):
        ref = weights.at[r, x, c, core]
        pltpu.make_async_copy(ref, ref, load_sem.at[r]).wait()

    def start_plane(r):
        wait_load(r)

        def step(j, carry):
            ref = weights.at[r, x, c, core]
            remote(ref, ref, plane_send.at[r], plane_recv.at[r], (m, lax.rem(c + j, 16))).start()
            return carry
        lax.fori_loop(1, 16, step, 0)

    def plane_bytes(r, sem):
        ref = weights.at[r, x, 0:15, core]
        return pltpu.make_async_copy(ref, ref, sem.at[r])

    def line_copy(r, part, k):
        low, high = PARTS[part]
        ref = weights.at[r, x, :, core, low:high]
        return remote(ref, ref, line_send.at[r, part, k - 1], line_recv.at[r, part, k - 1], line(k))

    def half_copy(r, part, k):
        low, high = PARTS[part]
        half = pl.ds(0, 8) if k == 1 else pl.ds(8, 8)
        ref = weights.at[r, along(-k), half, core, low:high]
        return remote(ref, ref, half_send.at[r, part, k - 1], half_recv.at[r, part, k - 1], line(k))

    def side_copy(r, part, k):
        low, high = PARTS[part]
        ref = weights.at[r, along(-k), :, core, low:high]
        return remote(ref, ref, side_send.at[r, part, k], side_recv.at[r, part, k], sibling)

    def start_line(r):
        plane_bytes(r, plane_recv).wait()
        for part in range(2):
            for k in (1, 3):
                line_copy(r, part, k).start()
        for part in range(2):
            side_copy(r, part, 0).start()

    def pass_on(r, part):
        for k in (1, 3):
            line_copy(r, part, k).wait_recv()
            half_copy(r, part, k).start()
            side_copy(r, part, k).start()

    def finish_line(r, part):
        for k in (1, 3):
            half_copy(r, part, k).wait_recv()
        side_copy(r, part, 2).start()

    def wait_side(r, part):
        for k in range(4):
            side_copy(r, part, k).wait_recv()

    def matrix(r, i):
        return jnp.concatenate([weights[r, b, :, :, i].reshape(WIDTH, 128) for b in range(4)], axis=1)

    def slot_copy(k):
        src = own_slots.at[pl.ds(pl.multiple_of(along(k) * PLANE, PLANE), PLANE)]
        return remote(src, line_slots.at[k], slot_send.at[k - 1], slot_recv.at[k - 1], line(k))

    def node_copy(r, k):
        src = node_ref if r == 0 else node_mid
        return remote(src, line_nodes.at[r, k - 1], node_send.at[r, k - 1], node_recv.at[r, k - 1], line(k))

    sub = lax.broadcasted_iota(jnp.int32, (128, 128), 0)
    lane = lax.broadcasted_iota(jnp.int32, (128, 128), 1)
    lane_f = lane.astype(F32)
    at_slot = lane == lax.rem(sub, SLOT)

    def make_pick(k):
        def step(b, carry):
            which = lax.broadcasted_iota(jnp.int32, (128, PLANE), 1)
            row = lax.broadcasted_iota(jnp.int32, (128, PLANE), 0)
            spread = mm(hot(which == 8 * b + row // SLOT), line_slots[k])
            index = jnp.sum(jnp.where(at_slot, spread, 0.0), axis=1, keepdims=True)
            pick_send[k, pl.ds(pl.multiple_of(b * 128, 128), 128), :] = hot(index == lane_f)
            return carry
        lax.fori_loop(0, 4, step, 0)

    def gather(r, k):
        if k:
            nodes = line_nodes[r, k - 1]
        else:
            nodes = node_ref[...] if r == 0 else node_mid[...]
        outgoing[k] = mm(pick_send[k], nodes).astype(BF16)

    def landing(r, k):
        at = ((along(-k) * 2 + core) * 16 + c) * SLOT
        return table.at[r, pl.ds(pl.multiple_of(at, SLOT), SLOT)]

    def send(r, k):
        for side in range(2):
            def step(j, carry):
                chan = lax.rem(c + j, 16)
                to_core = lax.rem(core + side, 2)
                q = to_core * 16 + chan
                src = outgoing.at[k, pl.ds(pl.multiple_of(q * SLOT, SLOT), SLOT)]
                remote(
                    src, landing(r, k), ex_send.at[r, k, side], ex_recv.at[r, k, side], (x * 2 + to_core, chan)
                ).start()
                return carry
            lax.fori_loop(1 - side, 16, step, 0)
        if k:
            landing(r, k)[...] = outgoing[k, pl.ds(pl.multiple_of(own * SLOT, SLOT), SLOT), :]
        else:
            landing(r, k)[...] = jnp.zeros((SLOT, WIDTH), BF16)

    def wait_exchange(sem, r, k, side):
        ref = outgoing.at[0, pl.ds(0, (15 + side) * SLOT)]
        pltpu.make_async_copy(ref, ref, sem.at[r, k, side]).wait()

    for small in smalls:
        small.wait()
    slots = jnp.concatenate([slots_ref[...].astype(F32), jnp.zeros((128 - SLOT, 128), F32)], axis=0)
    own_slots[...] = jnp.transpose(slots).astype(BF16)
    line_slots[0] = own_slots[pl.ds(pl.multiple_of(x * PLANE, PLANE), PLANE), :]
    make_pick(0)
    gather(0, 0)

    pl.semaphore_wait(barrier, 19)
    pl.semaphore_signal(ready, inc=1, device_id=sibling, device_id_type=MESH)
    for k in ORDER:
        slot_copy(k).start()
        node_copy(0, k).start()
    start_plane(0)
    pl.semaphore_wait(ready, 1)
    send(0, 0)

    eye = sub == lane
    ones = jnp.ones((128, 128), BF16)

    def column(row):
        wide = jnp.broadcast_to(row.astype(F32), (128, 128))
        return mm(jnp.where(eye, wide, 0.0).astype(BF16), ones)

    def edge_block(i, carry):
        rows = pl.ds(pl.multiple_of(i * 128, 128), 128)
        sender = sender_ref[pl.ds(i, 1), :]
        receiver = receiver_ref[pl.ds(i, 1), :]
        index = column(lax.shift_right_logical(sender, 7)) * 128.0 + column(sender & 127)
        pick_local[rows, :] = hot(index == lane_f)
        for j in range(16):
            pick_sender[j // 4, rows, (j % 4) * 128:(j % 4 + 1) * 128] = hot(index == lane_f + 128.0 * (j + 1))
        pick_receiver[rows, :] = hot(column(receiver) == lane_f)
        sum_receiver[:, rows] = hot(receiver == sub)
        return carry

    def relay(r, k):
        node_copy(r, k).wait_recv()
        gather(r, k)
        send(r, k)

    def tiles(step):
        for t in range(EDGE // TILE):
            step(slice(t * TILE, (t + 1) * TILE))

    def picked(r, k, rows):
        source = along(-k)
        block = table[r, pl.ds(pl.multiple_of(source * PLANE_ROWS, PLANE_ROWS), PLANE_ROWS), :]
        return mm(pick_sender[source, rows, :], block)

    def arrive(r, k):
        nodes = node_ref if r == 0 else node_mid
        for side in range(2):
            wait_exchange(ex_recv, r, k, side)

        def step(rows):
            if k == 0:
                gathered[rows, :] = mm(pick_local[rows, :], nodes[...]) + picked(r, k, rows)
            else:
                gathered[rows, :] += picked(r, k, rows)
        tiles(step)

    def before(r):
        nodes = node_ref if r == 0 else node_mid
        wait_side(r, 0)
        recv_proj = mm(nodes[...], matrix(r, 2)).astype(BF16)

        def step(rows):
            total = mm(edges[rows, :], matrix(r, 0)) + mm(pick_receiver[rows, :], recv_proj)
            base[rows, :] = total + mm(gathered[rows, :].astype(BF16), matrix(r, 1))
        tiles(step)

    def after(r, k):
        source = along(-k)
        half = PLANE_ROWS // 2
        for side in range(2):
            wait_exchange(ex_recv, r, k, side)
            at = lax.rem(core + side, 2) * half
            block = table[r, pl.ds(pl.multiple_of(source * PLANE_ROWS + at, half), half), :]
            projected[pl.ds(pl.multiple_of(at, half), half), :] = mm(block, matrix(r, 1)).astype(BF16)

        def step(rows):
            preact = base[rows, :] + mm(pick_sender[source, rows, :], projected[...])
            output = mm(silu(preact).astype(BF16), matrix(r, 3))
            edges[rows, :] = (edges[rows, :].astype(F32) + norm_rows(output)).astype(BF16)
        tiles(step)

    def update(r):
        nodes = node_ref if r == 0 else node_mid
        wait_side(r, 1)
        total = mm(sum_receiver[...], edges[...]).astype(BF16)
        preact = mm(nodes[...], matrix(r, 4)) + mm(total, matrix(r, 5))
        output = mm(silu(preact).astype(BF16), matrix(r, 6))
        return (nodes[...].astype(F32) + norm_rows(output)).astype(BF16)

    lax.fori_loop(0, EDGE // 128, edge_block, 0)
    for k in ORDER:
        slot_copy(k).wait_recv()
        make_pick(k)
    start_line(0)
    relay(0, 1)
    relay(0, 3)
    pass_on(0, 0)
    relay(0, 2)
    start_plane(1)
    pass_on(0, 1)
    arrive(0, 0)
    finish_line(0, 0)
    arrive(0, 1)
    arrive(0, 3)
    pltpu.make_async_copy(edge_ref, edges, edge_sem.at[0]).wait()
    before(0)
    finish_line(0, 1)
    after(0, 2)
    node_mid[...] = update(0)

    for k in ORDER:
        node_copy(1, k).start()
    for k in range(4):
        for side in range(2):
            wait_exchange(ex_send, 0, k, side)
    gather(1, 0)
    send(1, 0)
    start_line(1)
    for k in ORDER:
        relay(1, k)
    pass_on(1, 0)
    arrive(1, 0)
    pass_on(1, 1)
    arrive(1, 1)
    finish_line(1, 0)
    arrive(1, 3)
    before(1)
    finish_line(1, 1)
    after(1, 2)
    pltpu.make_async_copy(edges, edge_out_ref, edge_sem.at[1]).start()
    node_out_ref[...] = update(1)

    for k in range(4):
        for side in range(2):
            wait_exchange(ex_send, 1, k, side)
    pltpu.make_async_copy(edges, edge_out_ref, edge_sem.at[1]).wait()
    for r in range(2):
        plane_bytes(r, plane_send).wait()
        for k in ORDER:
            node_copy(r, k).wait_send()
        for part in range(2):
            for k in (1, 3):
                line_copy(r, part, k).wait_send()
                half_copy(r, part, k).wait_send()
            for k in range(4):
                side_copy(r, part, k).wait_send()
    for k in ORDER:
        slot_copy(k).wait_send()


def hand_out(node_ref, edge_ref, node_out_ref, edge_out_ref, node_buf, edge_buf, sems):
    pieces = [(node_ref, node_buf, node_out_ref)]
    for i in range(4):
        rows = pl.ds(i * (EDGE // 4), EDGE // 4)
        pieces.append((edge_ref.at[rows], edge_buf.at[rows], edge_out_ref.at[rows]))
    loads = [pltpu.make_async_copy(src, buf, sems.at[0, i]) for i, (src, buf, _) in enumerate(pieces)]
    stores = [pltpu.make_async_copy(buf, dst, sems.at[1, i]) for i, (_, buf, dst) in enumerate(pieces)]
    for load in loads:
        load.start()
    for load, store in zip(loads, stores):
        load.wait()
        store.start()
    for store in stores:
        store.wait()


def local(node_latents, edge_latents, sender_slot, receiver_node, send_rows, edge_in, edge_out, node_in, node_out):
    vmem = pl.BlockSpec(memory_space=pltpu.VMEM)
    anywhere = pl.BlockSpec(memory_space=pl.ANY)
    dma = pltpu.SemaphoreType.DMA
    node_state, edge_state = pl.pallas_call(
        kernel,
        out_shape=(
            jax.ShapeDtypeStruct((NODE, WIDTH), BF16),
            jax.ShapeDtypeStruct((EDGE, WIDTH), BF16),
        ),
        in_specs=[anywhere] * 9,
        out_specs=(vmem, anywhere),
        scratch_shapes=[
            pltpu.VMEM((2, 4, 16, 2, 7, 16, 128), BF16),
            pltpu.VMEM((4, PLANE_ROWS, WIDTH), BF16),
            pltpu.VMEM((2, 4 * PLANE_ROWS, WIDTH), BF16),
            pltpu.VMEM((NODE, WIDTH), BF16),
            pltpu.VMEM((2, 3, NODE, WIDTH), BF16),
            pltpu.VMEM((128, 128), BF16),
            pltpu.VMEM((4, PLANE, 128), BF16),
            pltpu.VMEM((EDGE, NODE), BF16),
            pltpu.VMEM((4, EDGE, PLANE_ROWS), BF16),
            pltpu.VMEM((EDGE, NODE), BF16),
            pltpu.VMEM((NODE, EDGE), BF16),
            pltpu.VMEM((4, PLANE_ROWS, NODE), BF16),
            pltpu.VMEM((EDGE, WIDTH), F32),
            pltpu.VMEM((EDGE, WIDTH), F32),
            pltpu.VMEM((NODE, WIDTH), BF16),
            pltpu.VMEM((8, 128), jnp.int32),
            pltpu.VMEM((8, 128), jnp.int32),
            pltpu.VMEM((SLOT, 128), jnp.int32),
            pltpu.VMEM((EDGE, WIDTH), BF16),
            pltpu.VMEM((PLANE_ROWS, WIDTH), BF16),
            pltpu.SemaphoreType.REGULAR,
            dma((4,)),
            dma((2,)), dma((2,)), dma((2, 4, 2)), dma((2, 4, 2)), dma((2, 3)), dma((2, 3)), dma((3,)), dma((3,)),
            dma((2,)), dma((2,)), dma((2, 2, 3)), dma((2, 2, 3)), dma((2, 2, 3)), dma((2, 2, 3)), dma((2, 2, 4)), dma((2, 2, 4)),
        ],
        compiler_params=pltpu.CompilerParams(
            collective_id=0, has_side_effects=True, vmem_limit_bytes=56 * 1024 * 1024
        ),
    )(
        node_latents,
        edge_latents,
        sender_slot.reshape(8, 128),
        receiver_node.reshape(8, 128),
        jnp.transpose(send_rows),
        edge_in.reshape(2, 3, 2, 16, WIDTH),
        edge_out.reshape(2, 2, 16, WIDTH),
        node_in.reshape(2, 2, 2, 16, WIDTH),
        node_out.reshape(2, 2, 16, WIDTH),
    )
    return pl.pallas_call(
        hand_out,
        out_shape=(
            jax.ShapeDtypeStruct((NODE, WIDTH), BF16),
            jax.ShapeDtypeStruct((EDGE, WIDTH), BF16),
        ),
        in_specs=[anywhere] * 2,
        out_specs=(anywhere, anywhere),
        scratch_shapes=[pltpu.VMEM((NODE, WIDTH), BF16), pltpu.VMEM((EDGE, WIDTH), BF16), dma((2, 5))],
    )(node_state, edge_state)


def solution(mesh):
    rows = P(("mesh", "chan"), None)
    flat = P(("mesh", "chan"))
    return jax.shard_map(
        local,
        mesh=mesh,
        in_specs=(
            rows, rows, flat, flat, rows,
            P(None, None, "chan", None), P(None, "chan", None),
            P(None, None, "chan", None), P(None, "chan", None),
        ),
        out_specs=(rows, rows),
        check_vma=False,
    )
```

```python
import jax
import jax.numpy as jnp
from jax import lax
from jax.experimental import pallas as pl
from jax.experimental.pallas import tpu as pltpu
from jax.sharding import PartitionSpec as P

MESH = pl.DeviceIdType.MESH
F32 = jnp.float32
BF16 = jnp.bfloat16
WIDTH = 512
NODE = 128
EDGE = 1024
SLOT = 16
PLANE = 32
PLANE_ROWS = PLANE * SLOT
TILE = 512
PARTS = ((0, 4), (4, 7))
ORDER = (1, 3, 2)


def mm(a, b):
    return jnp.dot(a, b, preferred_element_type=F32)


def hot(mask):
    return jnp.where(mask, 1.0, 0.0).astype(BF16)


def norm_rows(v):
    mean = jnp.sum(v, axis=1, keepdims=True) * (1.0 / WIDTH)
    square = jnp.sum(v * v, axis=1, keepdims=True) * (1.0 / WIDTH)
    return (v - mean) * lax.rsqrt(square - mean * mean + 1e-05)


def silu(v):
    half = 0.5 * v
    return half + half * jnp.tanh(half)


def kernel(
    node_in, edge_ref, sender_in, receiver_in, slots_in, ein, eout, nin, nout,
    node_out_ref, edge_out_ref,
    weights, outgoing, table, node_mid, line_nodes, own_slots, line_slots,
    pick_local, pick_sender, pick_receiver, sum_receiver, pick_send, base, gathered,
    node_ref, sender_ref, receiver_ref, slots_ref, edges, projected, ready, small_sem, edge_sem, load_sem, ex_send, ex_recv, node_send, node_recv, slot_send, slot_recv,
    plane_send, plane_recv, line_send, line_recv, half_send, half_recv, side_send, side_recv,
):
    m = lax.axis_index("mesh")
    c = lax.axis_index("chan")
    x, core = m // 2, lax.rem(m, 2)
    own = core * 16 + c
    sibling = (x * 2 + 1 - core, c)

    def along(k):
        return lax.rem(x + k + 4, 4)

    def line(k):
        return (along(k) * 2 + core, c)

    barrier = pltpu.get_barrier_semaphore()
    def greet(j, carry):
        pl.semaphore_signal(barrier, inc=1, device_id=(m, lax.rem(c + j, 16)), device_id_type=MESH)
        return carry

    lax.fori_loop(1, 16, greet, 0)
    for k in (2, 1, 3):
        pl.semaphore_signal(barrier, inc=1, device_id=line(k), device_id_type=MESH)
    pl.semaphore_signal(barrier, inc=1, device_id=sibling, device_id_type=MESH)
    smalls = [
        pltpu.make_async_copy(src, dst, small_sem.at[i])
        for i, (src, dst) in enumerate(
            ((slots_in, slots_ref), (node_in, node_ref), (sender_in, sender_ref), (receiver_in, receiver_ref))
        )
    ]
    for small in smalls:
        small.start()
    pltpu.make_async_copy(edge_ref, edges, edge_sem.at[0]).start()

    columns = pl.ds(pl.multiple_of(x * 128, 128), 128)
    for r in range(2):
        for src, low, high in (
            (ein.at[r, :, core, :, columns], 0, 3),
            (eout.at[pl.ds(r, 1), core, :, columns], 3, 4),
            (nin.at[r, :, core, :, columns], 4, 6),
            (nout.at[pl.ds(r, 1), core, :, columns], 6, 7),
        ):
            pltpu.make_async_copy(src, weights.at[r, x, c, core, low:high], load_sem.at[r]).start()

    def remote(src, dst, send, recv, device):
        return pltpu.make_async_remote_copy(
            src_ref=src, dst_ref=dst, send_sem=send, recv_sem=recv, device_id=device, device_id_type=MESH
        )

    def wait_load(r):
        ref = weights.at[r, x, c, core]
        pltpu.make_async_copy(ref, ref, load_sem.at[r]).wait()

    def start_plane(r):
        wait_load(r)

        def step(j, carry):
            ref = weights.at[r, x, c, core]
            remote(ref, ref, plane_send.at[r], plane_recv.at[r], (m, lax.rem(c + j, 16))).start()
            return carry
        lax.fori_loop(1, 16, step, 0)

    def plane_bytes(r, sem):
        ref = weights.at[r, x, 0:15, core]
        return pltpu.make_async_copy(ref, ref, sem.at[r])

    def line_copy(r, part, k):
        low, high = PARTS[part]
        ref = weights.at[r, x, :, core, low:high]
        return remote(ref, ref, line_send.at[r, part, k - 1], line_recv.at[r, part, k - 1], line(k))

    def half_copy(r, part, k):
        low, high = PARTS[part]
        half = pl.ds(0, 8) if k == 1 else pl.ds(8, 8)
        ref = weights.at[r, along(-k), half, core, low:high]
        return remote(ref, ref, half_send.at[r, part, k - 1], half_recv.at[r, part, k - 1], line(k))

    def side_copy(r, part, k):
        low, high = PARTS[part]
        ref = weights.at[r, along(-k), :, core, low:high]
        return remote(ref, ref, side_send.at[r, part, k], side_recv.at[r, part, k], sibling)

    def start_line(r):
        plane_bytes(r, plane_recv).wait()
        for part in range(2):
            for k in (1, 3):
                line_copy(r, part, k).start()
        for part in range(2):
            side_copy(r, part, 0).start()

    def pass_on(r, part):
        for k in (1, 3):
            line_copy(r, part, k).wait_recv()
            half_copy(r, part, k).start()
            side_copy(r, part, k).start()

    def finish_line(r, part):
        for k in (1, 3):
            half_copy(r, part, k).wait_recv()
        side_copy(r, part, 2).start()

    def wait_side(r, part):
        for k in range(4):
            side_copy(r, part, k).wait_recv()

    def matrix(r, i):
        return jnp.concatenate([weights[r, b, :, :, i].reshape(WIDTH, 128) for b in range(4)], axis=1)

    def slot_copy(k):
        src = own_slots.at[pl.ds(pl.multiple_of(along(k) * PLANE, PLANE), PLANE)]
        return remote(src, line_slots.at[k], slot_send.at[k - 1], slot_recv.at[k - 1], line(k))

    def node_copy(r, k):
        src = node_ref if r == 0 else node_mid
        return remote(src, line_nodes.at[r, k - 1], node_send.at[r, k - 1], node_recv.at[r, k - 1], line(k))

    sub = lax.broadcasted_iota(jnp.int32, (128, 128), 0)
    lane = lax.broadcasted_iota(jnp.int32, (128, 128), 1)
    lane_f = lane.astype(F32)
    at_slot = lane == lax.rem(sub, SLOT)

    def make_pick(k):
        def step(b, carry):
            which = lax.broadcasted_iota(jnp.int32, (128, PLANE), 1)
            row = lax.broadcasted_iota(jnp.int32, (128, PLANE), 0)
            spread = mm(hot(which == 8 * b + row // SLOT), line_slots[k])
            index = jnp.sum(jnp.where(at_slot, spread, 0.0), axis=1, keepdims=True)
            pick_send[k, pl.ds(pl.multiple_of(b * 128, 128), 128), :] = hot(index == lane_f)
            return carry
        lax.fori_loop(0, 4, step, 0)

    def gather(r, k):
        if k:
            nodes = line_nodes[r, k - 1]
        else:
            nodes = node_ref[...] if r == 0 else node_mid[...]
        outgoing[k] = mm(pick_send[k], nodes).astype(BF16)

    def landing(r, k):
        at = ((along(-k) * 2 + core) * 16 + c) * SLOT
        return table.at[r, pl.ds(pl.multiple_of(at, SLOT), SLOT)]

    def send(r, k):
        for side in range(2):
            def step(j, carry):
                chan = lax.rem(c + j, 16)
                to_core = lax.rem(core + side, 2)
                q = to_core * 16 + chan
                src = outgoing.at[k, pl.ds(pl.multiple_of(q * SLOT, SLOT), SLOT)]
                remote(
                    src, landing(r, k), ex_send.at[r, k, side], ex_recv.at[r, k, side], (x * 2 + to_core, chan)
                ).start()
                return carry
            lax.fori_loop(1 - side, 16, step, 0)
        if k:
            landing(r, k)[...] = outgoing[k, pl.ds(pl.multiple_of(own * SLOT, SLOT), SLOT), :]
        else:
            landing(r, k)[...] = jnp.zeros((SLOT, WIDTH), BF16)

    def wait_exchange(sem, r, k, side):
        ref = outgoing.at[0, pl.ds(0, (15 + side) * SLOT)]
        pltpu.make_async_copy(ref, ref, sem.at[r, k, side]).wait()

    for small in smalls:
        small.wait()
    slots = jnp.concatenate([slots_ref[...].astype(F32), jnp.zeros((128 - SLOT, 128), F32)], axis=0)
    own_slots[...] = jnp.transpose(slots).astype(BF16)
    line_slots[0] = own_slots[pl.ds(pl.multiple_of(x * PLANE, PLANE), PLANE), :]
    make_pick(0)
    gather(0, 0)

    pl.semaphore_wait(barrier, 19)
    pl.semaphore_signal(ready, inc=1, device_id=sibling, device_id_type=MESH)
    for k in ORDER:
        slot_copy(k).start()
        node_copy(0, k).start()
    start_plane(0)
    pl.semaphore_wait(ready, 1)
    send(0, 0)

    eye = sub == lane
    ones = jnp.ones((128, 128), BF16)

    def column(row):
        wide = jnp.broadcast_to(row.astype(F32), (128, 128))
        return mm(jnp.where(eye, wide, 0.0).astype(BF16), ones)

    def edge_block(i, carry):
        rows = pl.ds(pl.multiple_of(i * 128, 128), 128)
        sender = sender_ref[pl.ds(i, 1), :]
        receiver = receiver_ref[pl.ds(i, 1), :]
        index = column(lax.shift_right_logical(sender, 7)) * 128.0 + column(sender & 127)
        pick_local[rows, :] = hot(index == lane_f)
        for j in range(16):
            pick_sender[j // 4, rows, (j % 4) * 128:(j % 4 + 1) * 128] = hot(index == lane_f + 128.0 * (j + 1))
        pick_receiver[rows, :] = hot(column(receiver) == lane_f)
        sum_receiver[:, rows] = hot(receiver == sub)
        return carry

    def relay(r, k):
        if r == 0:
            slot_copy(k).wait_recv()
            make_pick(k)
        node_copy(r, k).wait_recv()
        gather(r, k)
        send(r, k)

    def tiles(step):
        for t in range(EDGE // TILE):
            step(slice(t * TILE, (t + 1) * TILE))

    def picked(r, k, rows):
        source = along(-k)
        block = table[r, pl.ds(pl.multiple_of(source * PLANE_ROWS, PLANE_ROWS), PLANE_ROWS), :]
        return mm(pick_sender[source, rows, :], block)

    def arrive(r, k):
        nodes = node_ref if r == 0 else node_mid
        for side in range(2):
            wait_exchange(ex_recv, r, k, side)

        def step(rows):
            if k == 0:
                gathered[rows, :] = mm(pick_local[rows, :], nodes[...]) + picked(r, k, rows)
            else:
                gathered[rows, :] += picked(r, k, rows)
        tiles(step)

    def before(r):
        nodes = node_ref if r == 0 else node_mid
        wait_side(r, 0)
        recv_proj = mm(nodes[...], matrix(r, 2)).astype(BF16)

        def step(rows):
            total = mm(edges[rows, :], matrix(r, 0)) + mm(pick_receiver[rows, :], recv_proj)
            base[rows, :] = total + mm(gathered[rows, :].astype(BF16), matrix(r, 1))
        tiles(step)

    def after(r, k):
        source = along(-k)
        half = PLANE_ROWS // 2
        for side in range(2):
            wait_exchange(ex_recv, r, k, side)
            at = lax.rem(core + side, 2) * half
            block = table[r, pl.ds(pl.multiple_of(source * PLANE_ROWS + at, half), half), :]
            projected[pl.ds(pl.multiple_of(at, half), half), :] = mm(block, matrix(r, 1)).astype(BF16)

        def step(rows):
            preact = base[rows, :] + mm(pick_sender[source, rows, :], projected[...])
            output = mm(silu(preact).astype(BF16), matrix(r, 3))
            edges[rows, :] = (edges[rows, :].astype(F32) + norm_rows(output)).astype(BF16)
        tiles(step)

    def update(r):
        nodes = node_ref if r == 0 else node_mid
        wait_side(r, 1)
        total = mm(sum_receiver[...], edges[...]).astype(BF16)
        preact = mm(nodes[...], matrix(r, 4)) + mm(total, matrix(r, 5))
        output = mm(silu(preact).astype(BF16), matrix(r, 6))
        return (nodes[...].astype(F32) + norm_rows(output)).astype(BF16)

    lax.fori_loop(0, EDGE // 128, edge_block, 0)
    start_line(0)
    relay(0, 1)
    relay(0, 3)
    pass_on(0, 0)
    relay(0, 2)
    start_plane(1)
    pass_on(0, 1)
    arrive(0, 0)
    finish_line(0, 0)
    finish_line(0, 1)
    arrive(0, 1)
    arrive(0, 3)
    pltpu.make_async_copy(edge_ref, edges, edge_sem.at[0]).wait()
    before(0)
    after(0, 2)
    node_mid[...] = update(0)

    for k in ORDER:
        node_copy(1, k).start()
    for k in range(4):
        for side in range(2):
            wait_exchange(ex_send, 0, k, side)
    gather(1, 0)
    send(1, 0)
    start_line(1)
    for k in ORDER:
        relay(1, k)
    pass_on(1, 0)
    arrive(1, 0)
    pass_on(1, 1)
    arrive(1, 1)
    finish_line(1, 0)
    arrive(1, 3)
    finish_line(1, 1)
    before(1)
    after(1, 2)
    pltpu.make_async_copy(edges, edge_out_ref, edge_sem.at[1]).start()
    node_out_ref[...] = update(1)

    for k in range(4):
        for side in range(2):
            wait_exchange(ex_send, 1, k, side)
    pltpu.make_async_copy(edges, edge_out_ref, edge_sem.at[1]).wait()
    for r in range(2):
        plane_bytes(r, plane_send).wait()
        for k in ORDER:
            node_copy(r, k).wait_send()
        for part in range(2):
            for k in (1, 3):
                line_copy(r, part, k).wait_send()
                half_copy(r, part, k).wait_send()
            for k in range(4):
                side_copy(r, part, k).wait_send()
    for k in ORDER:
        slot_copy(k).wait_send()


def hand_out(node_ref, edge_ref, node_out_ref, edge_out_ref, node_buf, edge_buf, sems):
    pieces = [(node_ref, node_buf, node_out_ref)]
    for i in range(8):
        rows = pl.ds(i * (EDGE // 8), EDGE // 8)
        pieces.append((edge_ref.at[rows], edge_buf.at[rows], edge_out_ref.at[rows]))
    loads = [pltpu.make_async_copy(src, buf, sems.at[0, i]) for i, (src, buf, _) in enumerate(pieces)]
    stores = [pltpu.make_async_copy(buf, dst, sems.at[1, i]) for i, (_, buf, dst) in enumerate(pieces)]
    for load in loads:
        load.start()
    for load, store in zip(loads, stores):
        load.wait()
        store.start()
    for store in stores:
        store.wait()


def local(node_latents, edge_latents, sender_slot, receiver_node, send_rows, edge_in, edge_out, node_in, node_out):
    vmem = pl.BlockSpec(memory_space=pltpu.VMEM)
    anywhere = pl.BlockSpec(memory_space=pl.ANY)
    dma = pltpu.SemaphoreType.DMA
    node_state, edge_state = pl.pallas_call(
        kernel,
        out_shape=(
            jax.ShapeDtypeStruct((NODE, WIDTH), BF16),
            jax.ShapeDtypeStruct((EDGE, WIDTH), BF16),
        ),
        in_specs=[anywhere] * 9,
        out_specs=(vmem, anywhere),
        scratch_shapes=[
            pltpu.VMEM((2, 4, 16, 2, 7, 16, 128), BF16),
            pltpu.VMEM((4, PLANE_ROWS, WIDTH), BF16),
            pltpu.VMEM((2, 4 * PLANE_ROWS, WIDTH), BF16),
            pltpu.VMEM((NODE, WIDTH), BF16),
            pltpu.VMEM((2, 3, NODE, WIDTH), BF16),
            pltpu.VMEM((128, 128), BF16),
            pltpu.VMEM((4, PLANE, 128), BF16),
            pltpu.VMEM((EDGE, NODE), BF16),
            pltpu.VMEM((4, EDGE, PLANE_ROWS), BF16),
            pltpu.VMEM((EDGE, NODE), BF16),
            pltpu.VMEM((NODE, EDGE), BF16),
            pltpu.VMEM((4, PLANE_ROWS, NODE), BF16),
            pltpu.VMEM((EDGE, WIDTH), F32),
            pltpu.VMEM((EDGE, WIDTH), F32),
            pltpu.VMEM((NODE, WIDTH), BF16),
            pltpu.VMEM((8, 128), jnp.int32),
            pltpu.VMEM((8, 128), jnp.int32),
            pltpu.VMEM((SLOT, 128), jnp.int32),
            pltpu.VMEM((EDGE, WIDTH), BF16),
            pltpu.VMEM((PLANE_ROWS, WIDTH), BF16),
            pltpu.SemaphoreType.REGULAR,
            dma((4,)),
            dma((2,)), dma((2,)), dma((2, 4, 2)), dma((2, 4, 2)), dma((2, 3)), dma((2, 3)), dma((3,)), dma((3,)),
            dma((2,)), dma((2,)), dma((2, 2, 3)), dma((2, 2, 3)), dma((2, 2, 3)), dma((2, 2, 3)), dma((2, 2, 4)), dma((2, 2, 4)),
        ],
        compiler_params=pltpu.CompilerParams(
            collective_id=0, has_side_effects=True, vmem_limit_bytes=56 * 1024 * 1024
        ),
    )(
        node_latents,
        edge_latents,
        sender_slot.reshape(8, 128),
        receiver_node.reshape(8, 128),
        jnp.transpose(send_rows),
        edge_in.reshape(2, 3, 2, 16, WIDTH),
        edge_out.reshape(2, 2, 16, WIDTH),
        node_in.reshape(2, 2, 2, 16, WIDTH),
        node_out.reshape(2, 2, 16, WIDTH),
    )
    return pl.pallas_call(
        hand_out,
        out_shape=(
            jax.ShapeDtypeStruct((NODE, WIDTH), BF16),
            jax.ShapeDtypeStruct((EDGE, WIDTH), BF16),
        ),
        in_specs=[anywhere] * 2,
        out_specs=(anywhere, anywhere),
        scratch_shapes=[pltpu.VMEM((NODE, WIDTH), BF16), pltpu.VMEM((EDGE, WIDTH), BF16), dma((2, 9))],
    )(node_state, edge_state)


def solution(mesh):
    rows = P(("mesh", "chan"), None)
    flat = P(("mesh", "chan"))
    return jax.shard_map(
        local,
        mesh=mesh,
        in_specs=(
            rows, rows, flat, flat, rows,
            P(None, None, "chan", None), P(None, "chan", None),
            P(None, None, "chan", None), P(None, "chan", None),
        ),
        out_specs=(rows, rows),
        check_vma=False,
    )
```
